32 devices in a mesh: dp: 8 (over y, x, core), tensor: 4 (over z).
Axes of the slice: x: 2, y: 2, z: 4, core: 2. Of those that a mesh axis runs over, the one named last changes fastest.
Arguments:
- tokens: bfloat16 [6, 4096, 4096], P(None, 'dp', 'tensor'), may hold values from -16 to 16
- router: bfloat16 [16, 4096], P(None, 'tensor'), may hold values from -32 to 32
- w_gate: bfloat16 [4, 14336, 4096], P('tensor', 'dp'), may hold values from -0.625 to 0.625
- w_up: bfloat16 [4, 14336, 4096], P('tensor', 'dp'), may hold values from -0.625 to 0.625
- w_down: bfloat16 [4, 14336, 4096], P('tensor', 'dp'), may hold values from -0.046875 to 0.046875
Outputs:
- mixed: bfloat16 [6, 4096, 4096], P(None, 'dp', 'tensor')
- log_total: float32 [6, 4096], P(None, 'dp')
The draws below stay inside these ranges and needn't reach their ends.
All inputs are finite; a program needn't handle non-finite values.
Results may differ from the reference program's by a relative error of at most 0.0096.
Values may be sent and summed in bfloat16 or wider, within the bound.
A program may use at most 128 MiB of HBM per device.

```python
import math
import jax
import jax.numpy as jnp
from jax import lax

D = 4096
FF = 14336
SLOTS = 4
GROUPS = 6
EW = 4
WS = 16
TOKENS = 4096


def shared_base(key):
    return jnp.clip(jax.random.normal(key, (WS, D), jnp.float32), -5.0, 5.0)


def draw_tokens(key, part):
    key = jax.random.fold_in(key, 11)
    first_key = jax.random.fold_in(key, 0)
    position = jnp.arange(D, dtype=jnp.float32)
    rising = jnp.exp(0.5 * math.log(3.0) * position / max(D - 1, 1))
    normals = jax.random.normal(first_key, (GROUPS, TOKENS, D), jnp.float32)
    values = jnp.clip(normals * rising, -16.0, 16.0)
    return values.astype(jnp.bfloat16)


def draw_router(key, part):
    anchors = shared_base(key)
    key = jax.random.fold_in(key, 23)
    first_key = jax.random.fold_in(key, 0)
    spread = jnp.exp(jax.random.uniform(first_key, (WS, 1), jnp.float32, math.log(4.0), math.log(5.0)))
    router_rows = anchors * spread / math.sqrt(D)
    return jnp.clip(router_rows, -32.0, 32.0).astype(jnp.bfloat16)


def shard_levels(rng, shape, cuts, smallest, top_value):
    factor_of, own = 1.0, jax.random.fold_in(rng, 6)
    for axis_at, blocks in cuts:
        steps = jnp.exp(jax.random.uniform(jax.random.fold_in(own, axis_at), (blocks,), jnp.float32, smallest / len(cuts), top_value / len(cuts)))
        factor_of = factor_of * jnp.repeat(steps, shape[axis_at] // blocks).reshape([-1 if axis == axis_at else 1 for axis in range(len(shape))])
    return factor_of


def normal_values(rng, shape, scale, limit, cuts=(), kind=jnp.bfloat16):
    factor_of = shard_levels(rng, shape, cuts, -0.22, 0.18) if cuts else 1.0
    entries = jax.random.normal(rng, shape, jnp.float32) * scale * factor_of
    return jnp.minimum(jnp.maximum(entries, -limit), limit).astype(kind)


def setup_inputs(seed: int = 0) -> dict:
    splits = jax.random.split(jax.random.key(seed), 6)
    return {
        "tokens": draw_tokens(jax.random.fold_in(splits[5], 71), 0),
        "router": draw_router(jax.random.fold_in(splits[5], 71), 0),
        "w_gate": normal_values(splits[2], (EW, FF, D), (D // 48) ** -0.5, 0.625, ((0, 4), (1, 8))),
        "w_up": normal_values(splits[3], (EW, FF, D), (D // 48) ** -0.5, 0.625, ((0, 4), (1, 8))),
        "w_down": normal_values(splits[4], (EW, FF, D), FF ** -0.5, 0.046875, ((0, 4), (1, 8))),
    }


epsilon = 1e-05

def front_group(group_rows, router):
    as_float = group_rows.astype(jnp.float32)
    norm_scale = lax.rsqrt(lax.optimization_barrier(jnp.mean(as_float * as_float, axis=1)) + epsilon)
    logits = jnp.dot(router, group_rows.T, preferred_element_type=jnp.float32) * norm_scale[None, :]
    column_peak = lax.optimization_barrier(jnp.max(logits, axis=1, keepdims=True))
    powers = jnp.exp(logits - column_peak)
    column_sum = lax.optimization_barrier(jnp.sum(powers, axis=1, keepdims=True))
    weights = (powers * norm_scale[None, :]).astype(jnp.bfloat16)
    slot_in = (jnp.dot(weights, group_rows, preferred_element_type=jnp.float32) / column_sum).astype(jnp.bfloat16)
    row_peak = lax.optimization_barrier(jnp.max(logits, axis=0, keepdims=True))
    row_powers = jnp.exp(logits - row_peak)
    row_sum = lax.optimization_barrier(jnp.sum(row_powers, axis=0, keepdims=True))
    combine = (row_powers / row_sum).astype(jnp.bfloat16)
    log_total = (row_peak + jnp.log(row_sum))[0]
    return (slot_in, combine, log_total)

def mix_group(paired):
    combine, slot_out = paired
    return jnp.dot(combine.T, slot_out, preferred_element_type=jnp.float32).astype(jnp.bfloat16)

def reference(tokens, router, w_gate, w_up, w_down):
    slot_in, combine, log_total = lax.map(lambda group_rows: front_group(group_rows, router), tokens)
    groups = tokens.shape[0]
    results = []
    for expert in range(w_gate.shape[0]):
        slot_rows = slot_in[:, expert * SLOTS:(expert + 1) * SLOTS, :].reshape(groups * SLOTS, D)
        gate_act = jnp.dot(slot_rows, w_gate[expert].T, preferred_element_type=jnp.float32)
        up_act = jnp.dot(slot_rows, w_up[expert].T, preferred_element_type=jnp.float32)
        hidden = (jax.nn.silu(gate_act) * up_act).astype(jnp.bfloat16)
        expert_out = jnp.dot(hidden, w_down[expert], preferred_element_type=jnp.float32).astype(jnp.bfloat16)
        results.append(expert_out.reshape(groups, SLOTS, D))
    slot_out = jnp.concatenate(results, axis=1)
    mixed = lax.map(mix_group, (combine, slot_out))
    return (mixed, log_total)
```

```python
import functools

import jax
import jax.numpy as jnp
from jax import lax
from jax.experimental import pallas as pl
from jax.experimental.pallas import tpu as pltpu
from jax.sharding import PartitionSpec as P

SLOTS = 4
PAD = 32
LANES = 128
CHUNKS = 2
WPARTS = 4
epsilon = 1e-05
f32 = jnp.float32
bf16 = jnp.bfloat16
MESH = pl.DeviceIdType.MESH
NT = (((1,), (1,)), ((), ()))
NN = (((1,), (0,)), ((), ()))


def dispatch_kernel(
    nd, nt, tokens, router, w_gate, w_up, w_down,
    window_out, combine_out, total_out,
    tok, wg, wu, wd, stat, stat_in, logit, stats, pbuf, rbuf, abuf, zin, xin, x_all, hidden,
    obuf, oin, bbuf, zout,
    tok_sem, w_sem,
    rs_s, rs_r, ag_s, ag_r, st_s, st_r, pr_s, pr_r, az_s, az_r, ax_s, ax_r,
    or_s, or_r, bz_s, bz_r, bx_s, bx_r,
):
    me_d, me_t = lax.axis_index("dp"), lax.axis_index("tensor")
    groups, count, width = tok.shape
    owners = width // LANES
    quarter = count // nt
    per = groups // CHUNKS
    full_width = width * nt
    hidden_here = wg.shape[0]
    wrows = hidden_here // WPARTS
    is_owner_all = nd == owners

    def token_copy(g):
        return pltpu.make_async_copy(tokens.at[g], tok.at[g], tok_sem.at[g])

    def weight_copy(m, p):
        src, dst = ((w_gate, wg), (w_up, wu), (w_down, wd))[m]
        rows = pl.ds(p * wrows, wrows)
        return pltpu.make_async_copy(src.at[rows, :], dst.at[rows, :], w_sem.at[m, p])

    def ring(me, n, fn):
        def step(k, c):
            fn(lax.rem(me + k, n))
            return c
        lax.fori_loop(1, n, step, 0)

    def other_tensor(fn):
        ring(me_t, nt, fn)

    def other_dp(fn):
        ring(me_d, nd, fn)

    def other_owners(fn):
        if is_owner_all:
            ring(me_d, nd, fn)
        else:
            def step(j, c):
                pl.when(j != me_d)(functools.partial(fn, j))
                return c
            lax.fori_loop(0, owners, step, 0)

    def if_owner(fn):
        if is_owner_all:
            fn()
        else:
            pl.when(me_d < owners)(fn)

    def send(src, dst, s, r, axis, to):
        return pltpu.make_async_remote_copy(
            src_ref=src, dst_ref=dst, send_sem=s, recv_sem=r,
            device_id={axis: to}, device_id_type=MESH)

    for g in range(groups):
        token_copy(g).start()

    barrier = pltpu.get_barrier_semaphore()
    other_tensor(lambda t: pl.semaphore_signal(
        barrier, inc=1, device_id={"tensor": t}, device_id_type=MESH))
    other_dp(lambda d: pl.semaphore_signal(
        barrier, inc=1, device_id={"dp": d}, device_id_type=MESH))

    ones = jnp.ones((8, LANES), f32)
    router_rows = router[...]

    for c in range(CHUNKS):
        def partial_logits(gl, carry, c=c):
            g = c * per + gl
            token_copy(g).wait()
            raw = lax.dot_general(router_rows, tok[g], NT, preferred_element_type=f32)
            rows = pl.ds(pl.multiple_of(gl * 16, 16), 16)
            for q in range(nt):
                stat[c, q, rows, :] = raw[:, q * quarter:(q + 1) * quarter]
                acc = jnp.zeros((quarter, LANES), f32)
                for b in range(owners):
                    part = tok[g, q * quarter:(q + 1) * quarter, b * LANES:(b + 1) * LANES].astype(f32)
                    acc = acc + part * part
                sq = lax.dot_general(ones, acc, NT, precision=lax.Precision.HIGHEST,
                                     preferred_element_type=f32)
                stat[c, q, pl.ds(per * 16 + gl, 1), :] = sq[0:1]
            return carry
        stat[c, :, per * 16:, :] = jnp.zeros((nt, 8, LANES), f32)
        lax.fori_loop(0, per, partial_logits, 0)
        if c == 0:
            pl.semaphore_wait(barrier, nt - 1 + nd - 1)
        other_tensor(lambda t, c=c: send(
            stat.at[c, t], stat_in.at[c, me_t], rs_s.at[c, t], rs_r.at[c, me_t], "tensor", t).start())
        if c == 0:
            for p in range(WPARTS):
                weight_copy(0, p).start()
    for m in (1, 2):
        for p in range(WPARTS):
            weight_copy(m, p).start()

    for c in range(CHUNKS):
        stat_in[c, me_t] = stat[c, me_t]
        other_tensor(lambda t, c=c: send(
            stat.at[c, t], stat_in.at[c, t], rs_s.at[c, t], rs_r.at[c, t], "tensor", t).wait_recv())
        total = stat_in[c, 0]
        for t in range(1, nt):
            total = total + stat_in[c, t]
        norm = lax.rsqrt(total[per * 16:] / full_width + epsilon)
        for gl in range(per):
            logit[c, me_t, gl * 16:(gl + 1) * 16, :] = total[gl * 16:(gl + 1) * 16] * norm[gl:gl + 1]
        logit[c, me_t, per * 16:, :] = norm
        other_tensor(lambda t, c=c: send(
            logit.at[c, me_t], logit.at[c, me_t], ag_s.at[c, t], ag_r.at[c, me_t], "tensor", t).start())

    stats[me_d] = jnp.ones(stats.shape[1:], f32)
    column = lax.broadcasted_iota(jnp.int32, (16, LANES), 1)
    for c in range(CHUNKS):
        other_tensor(lambda t, c=c: send(
            logit.at[c, t], logit.at[c, t], ag_s.at[c, t], ag_r.at[c, t], "tensor", t).wait_recv())

        def weigh(gl, carry, c=c):
            g = c * per + gl
            rows = pl.ds(pl.multiple_of(gl * 16, 16), 16)
            logits = jnp.concatenate([logit[c, q, rows, :] for q in range(nt)], axis=1)
            norm = jnp.concatenate([logit[c, q, pl.ds(per * 16 + gl, 1), :] for q in range(nt)], axis=1)
            peak = jnp.max(logits, axis=1, keepdims=True)
            powers = jnp.exp(logits - peak)
            csum = jnp.sum(powers, axis=1, keepdims=True)
            weights = (powers * norm).astype(bf16)
            summed = lax.dot_general(weights, tok[g], NN, preferred_element_type=f32)
            for j in range(owners):
                pbuf[c, j, gl] = summed[:, j * LANES:(j + 1) * LANES].astype(bf16)
            stats[me_d, 0] = jnp.where(column == g, peak, stats[me_d, 0])
            stats[me_d, 1] = jnp.where(column == g, csum, stats[me_d, 1])
            return carry
        lax.fori_loop(0, per, weigh, 0)
        if c == CHUNKS - 1:
            other_owners(lambda j: send(
                stats.at[me_d], stats.at[me_d], st_s.at[j], st_r.at[me_d], "dp", j).start())
        other_owners(lambda j, c=c: send(
            pbuf.at[c, j], rbuf.at[c, me_d], pr_s.at[c, j], pr_r.at[c, me_d], "dp", j).start())

    for c in range(CHUNKS):
        def mixing(gl, carry, c=c):
            g = c * per + gl
            rows = pl.ds(pl.multiple_of(gl * 16, 16), 16)
            logits = jnp.concatenate([logit[c, q, rows, :] for q in range(nt)], axis=1)
            row_peak = jnp.max(logits, axis=0, keepdims=True)
            row_powers = jnp.exp(logits - row_peak)
            row_sum = jnp.sum(row_powers, axis=0, keepdims=True)
            combine_out[g] = (row_powers / row_sum).astype(bf16)
            total_out[pl.ds(g, 1), :] = row_peak + jnp.log(row_sum)
            return carry
        lax.fori_loop(0, per, mixing, 0)

    def spread_matrix(rows, cols, flip):
        a = lax.broadcasted_iota(jnp.int32, (rows, cols), 1 if flip else 0)
        b = lax.broadcasted_iota(jnp.int32, (rows, cols), 0 if flip else 1)
        k, q = a // PAD, a % PAD
        source = (q // SLOTS) * 16 + k * SLOTS + q % SLOTS
        hit = jnp.logical_and(q < groups * SLOTS, source == b)
        return jnp.where(hit, 1.0, 0.0).astype(bf16)

    spread = spread_matrix(nt * PAD, groups * 16, False)
    gather = spread_matrix(groups * 16, nt * PAD, True)

    def reduce_slots():
        for c in range(CHUNKS):
            other_dp(lambda d, c=c: send(
                pbuf.at[c, 0], rbuf.at[c, d], pr_s.at[c, 0], pr_r.at[c, d], "dp", d).wait_recv())
            rbuf[c, me_d] = pbuf[c, me_d]
        other_dp(lambda d: send(
            stats.at[d], stats.at[d], st_s.at[0], st_r.at[d], "dp", d).wait_recv())
        peak = stats[0, 0]
        for i in range(1, nd):
            peak = jnp.maximum(peak, stats[i, 0])
        factor = [jnp.exp(stats[i, 0] - peak) for i in range(nd)]
        den = factor[0] * stats[0, 1]
        for i in range(1, nd):
            den = den + factor[i] * stats[i, 1]
        scale = [f / den for f in factor]
        rows = []
        for g in range(groups):
            c, gl = g // per, g % per
            acc = jnp.zeros((16, LANES), f32)
            for i in range(nd):
                acc = acc + scale[i][:, g:g + 1] * rbuf[c, i, gl].astype(f32)
            rows.append(acc.astype(bf16))
        slot_in = jnp.concatenate(rows, axis=0)
        moved = lax.dot_general(spread, slot_in, NN, preferred_element_type=f32).astype(bf16)
        for k in range(nt):
            abuf[k] = moved[k * PAD:(k + 1) * PAD]
        zin[me_t] = abuf[me_t]
        other_tensor(lambda t: send(
            abuf.at[t], zin.at[me_t], az_s.at[t], az_r.at[me_t], "tensor", t).start())
        other_tensor(lambda t: send(
            abuf.at[t], zin.at[t], az_s.at[t], az_r.at[t], "tensor", t).wait_recv())
        xin[me_d] = zin[...]
        other_dp(lambda d: send(
            zin, xin.at[me_d], ax_s.at[d], ax_r.at[me_d], "dp", d).start())
    if_owner(reduce_slots)
    other_owners(lambda j: send(
        zin, xin.at[j], ax_s.at[0], ax_r.at[j], "dp", j).wait_recv())

    for i in range(owners):
        for t in range(nt):
            x_all[:, t * width + i * LANES:t * width + (i + 1) * LANES] = xin[i, t]

    for m in (0, 1):
        for p in range(WPARTS):
            weight_copy(m, p).wait()
    fc = 256 if hidden_here % 256 == 0 else hidden_here

    def hidden_part(f, carry):
        at = pl.multiple_of(f * fc, fc)
        rows = pl.ds(at, fc)
        x = x_all[...]
        gate = lax.dot_general(x, wg[rows, :], NT, preferred_element_type=f32)
        up = lax.dot_general(x, wu[rows, :], NT, preferred_element_type=f32)
        act = gate / (1.0 + jnp.exp(-gate)) * up
        hidden[:, pl.ds(at, fc)] = act.astype(bf16)
        return carry
    lax.fori_loop(0, hidden_here // fc, hidden_part, 0)

    for p in range(WPARTS):
        weight_copy(2, p).wait()

    pairs = owners // 2

    def down_part(k, carry):
        p = lax.rem(k + me_d // 2 + 1, pairs)
        for t in range(nt):
            cols = pl.ds(pl.multiple_of(t * width + p * 2 * LANES, 2 * LANES), 2 * LANES)
            out = lax.dot_general(hidden[...], wd[:, cols], NN, preferred_element_type=f32)
            obuf[2 * p, t] = out[:, :LANES].astype(bf16)
            obuf[2 * p + 1, t] = out[:, LANES:].astype(bf16)
        for h in range(2):
            j = 2 * p + h

            @pl.when(j != me_d)
            def _():
                send(obuf.at[j], oin.at[me_d], or_s.at[j], or_r.at[me_d], "dp", j).start()
        return carry
    lax.fori_loop(0, pairs, down_part, 0)

    def reduce_outputs():
        oin[me_d] = obuf[me_d]
        other_dp(lambda d: send(
            obuf.at[0], oin.at[d], or_s.at[0], or_r.at[d], "dp", d).wait_recv())
        for t in range(nt):
            acc = oin[0, t].astype(f32)
            for i in range(1, nd):
                acc = acc + oin[i, t].astype(f32)
            bbuf[t] = acc.astype(bf16)
        zout[me_t] = bbuf[me_t]
        other_tensor(lambda t: send(
            bbuf.at[t], zout.at[me_t], bz_s.at[t], bz_r.at[me_t], "tensor", t).start())
        other_tensor(lambda t: send(
            bbuf.at[t], zout.at[t], bz_s.at[t], bz_r.at[t], "tensor", t).wait_recv())
        rows = jnp.concatenate([zout[k] for k in range(nt)], axis=0)
        window_out[me_d] = lax.dot_general(
            gather, rows, NN, preferred_element_type=f32).astype(bf16)
        other_dp(lambda d: send(
            window_out.at[me_d], window_out.at[me_d], bx_s.at[d], bx_r.at[me_d], "dp", d).start())
    if_owner(reduce_outputs)
    other_owners(lambda j: send(
        window_out.at[j], window_out.at[j], bx_s.at[0], bx_r.at[j], "dp", j).wait_recv())

    for c in range(CHUNKS):
        other_tensor(lambda t, c=c: send(
            stat.at[c, t], stat_in.at[c, t], rs_s.at[c, t], rs_r.at[c, t], "tensor", t).wait_send())
        other_tensor(lambda t, c=c: send(
            logit.at[c, me_t], logit.at[c, me_t], ag_s.at[c, t], ag_r.at[c, t], "tensor", t).wait_send())
        other_owners(lambda j, c=c: send(
            pbuf.at[c, j], rbuf.at[c, j], pr_s.at[c, j], pr_r.at[c, j], "dp", j).wait_send())
    other_owners(lambda j: send(
        stats.at[me_d], stats.at[me_d], st_s.at[j], st_r.at[j], "dp", j).wait_send())
    other_owners(lambda j: send(
        obuf.at[j], oin.at[j], or_s.at[j], or_r.at[j], "dp", j).wait_send())

    def drain():
        other_tensor(lambda t: send(
            abuf.at[t], zin.at[t], az_s.at[t], az_r.at[t], "tensor", t).wait_send())
        other_tensor(lambda t: send(
            bbuf.at[t], zout.at[t], bz_s.at[t], bz_r.at[t], "tensor", t).wait_send())
        other_dp(lambda d: send(
            zin, xin.at[0], ax_s.at[d], ax_r.at[d], "dp", d).wait_send())
        other_dp(lambda d: send(
            window_out.at[me_d], window_out.at[me_d], bx_s.at[d], bx_r.at[d], "dp", d).wait_send())
    if_owner(drain)


def mix_kernel(combine, window, total, mixed, total_out):
    slots = jnp.concatenate([window[j, 0] for j in range(window.shape[0])], axis=1)
    mixed[0] = lax.dot_general(
        combine[0], slots, (((0,), (0,)), ((), ())), preferred_element_type=f32).astype(bf16)
    total_out[...] = total[...]


def per_device(tokens, router, w_gate, w_up, w_down):
    nd, nt = lax.axis_size("dp"), lax.axis_size("tensor")
    groups, count, width = tokens.shape
    hidden_here, full = w_gate.shape[1:]
    slots = router.shape[0]
    owners = width // LANES
    quarter = count // nt
    per = groups // CHUNKS
    srows = per * 16 + 8
    VM, DMA = pltpu.VMEM, pltpu.SemaphoreType.DMA
    any_spec = pl.BlockSpec(memory_space=pl.ANY)
    vmem_spec = pl.BlockSpec(memory_space=pltpu.VMEM)
    window, combine, total = pl.pallas_call(
        functools.partial(dispatch_kernel, nd, nt),
        out_shape=(
            jax.ShapeDtypeStruct((owners, groups * slots, LANES), bf16),
            jax.ShapeDtypeStruct((groups, slots, count), bf16),
            jax.ShapeDtypeStruct((groups, count), f32),
        ),
        in_specs=[any_spec, vmem_spec, any_spec, any_spec, any_spec],
        out_specs=(vmem_spec, vmem_spec, vmem_spec),
        scratch_shapes=[
            VM((groups, count, width), bf16),
            VM((hidden_here, full), bf16),
            VM((hidden_here, full), bf16),
            VM((hidden_here, full), bf16),
            VM((CHUNKS, nt, srows, quarter), f32),
            VM((CHUNKS, nt, srows, quarter), f32),
            VM((CHUNKS, nt, srows, quarter), f32),
            VM((nd, 2, slots, LANES), f32),
            VM((CHUNKS, owners, per, slots, LANES), bf16),
            VM((CHUNKS, nd, per, slots, LANES), bf16),
            VM((nt, PAD, LANES), bf16),
            VM((nt, PAD, LANES), bf16),
            VM((owners, nt, PAD, LANES), bf16),
            VM((PAD, full), bf16),
            VM((PAD, hidden_here), bf16),
            VM((owners, nt, PAD, LANES), bf16),
            VM((nd, nt, PAD, LANES), bf16),
            VM((nt, PAD, LANES), bf16),
            VM((nt, PAD, LANES), bf16),
            DMA((groups,)), DMA((3, WPARTS)),
            DMA((CHUNKS, nt)), DMA((CHUNKS, nt)), DMA((CHUNKS, nt)), DMA((CHUNKS, nt)),
            DMA((owners,)), DMA((nd,)), DMA((CHUNKS, owners)), DMA((CHUNKS, nd)),
            DMA((nt,)), DMA((nt,)), DMA((nd,)), DMA((owners,)),
            DMA((owners,)), DMA((nd,)), DMA((nt,)), DMA((nt,)), DMA((nd,)), DMA((owners,)),
        ],
        compiler_params=pltpu.CompilerParams(
            collective_id=0, has_side_effects=True, vmem_limit_bytes=58 * 1024 * 1024),
        name="dispatch",
    )(tokens, router, w_gate[0], w_up[0], w_down[0])
    window = window.reshape(owners, groups, slots, LANES)
    mixed, log_total = pl.pallas_call(
        mix_kernel,
        grid=(groups,),
        out_shape=(
            jax.ShapeDtypeStruct((groups, count, width), bf16),
            jax.ShapeDtypeStruct((groups, count), f32),
        ),
        in_specs=[
            pl.BlockSpec((1, slots, count), lambda g: (g, 0, 0)),
            pl.BlockSpec((owners, 1, slots, LANES), lambda g: (0, g, 0, 0)),
            pl.BlockSpec((groups, count), lambda g: (0, 0)),
        ],
        out_specs=(
            pl.BlockSpec((1, count, width), lambda g: (g, 0, 0)),
            pl.BlockSpec((groups, count), lambda g: (0, 0)),
        ),
        name="mix",
    )(combine, window, total)
    return (mixed, log_total)


def solution(mesh):
    in_specs = (
        P(None, "dp", "tensor"),
        P(None, "tensor"),
        P("tensor", "dp", None),
        P("tensor", "dp", None),
        P("tensor", "dp", None),
    )
    out_specs = (P(None, "dp", "tensor"), P(None, "dp"))
    return jax.shard_map(
        per_device, mesh=mesh, in_specs=in_specs, out_specs=out_specs, check_vma=False
    )
```

```python
import functools

import jax
import jax.numpy as jnp
from jax import lax
from jax.experimental import pallas as pl
from jax.experimental.pallas import tpu as pltpu
from jax.sharding import PartitionSpec as P

SLOTS = 4
PAD = 32
LANES = 128
CHUNKS = 2
WPARTS = 4
epsilon = 1e-05
f32 = jnp.float32
bf16 = jnp.bfloat16
MESH = pl.DeviceIdType.MESH
NT = (((1,), (1,)), ((), ()))
NN = (((1,), (0,)), ((), ()))


def dispatch_kernel(
    nd, nt, tokens, router, w_gate, w_up, w_down,
    window_out, combine_out, total_out,
    tok, wg, wu, wd, stat, stat_in, wbuf, sbuf, stats, pbuf, rbuf, abuf, zin, xin, x_all, hidden,
    obuf, oin, bbuf, zout,
    tok_sem, w_sem,
    rs_s, rs_r, ag_s, ag_r, as_s, as_r, cb_s, cb_r, tb_s, tb_r, st_s, st_r, pr_s, pr_r, az_s, az_r, ax_s, ax_r,
    or_s, or_r, bz_s, bz_r, bx_s, bx_r,
):
    me_d, me_t = lax.axis_index("dp"), lax.axis_index("tensor")
    groups, count, width = tok.shape
    owners = width // LANES
    quarter = count // nt
    per = groups // CHUNKS
    full_width = width * nt
    hidden_here = wg.shape[0]
    wrows = hidden_here // WPARTS
    is_owner_all = nd == owners

    def token_copy(g):
        return pltpu.make_async_copy(tokens.at[g], tok.at[g], tok_sem.at[g])

    def weight_copy(m, p):
        src, dst = ((w_gate, wg), (w_up, wu), (w_down, wd))[m]
        rows = pl.ds(p * wrows, wrows)
        return pltpu.make_async_copy(src.at[rows, :], dst.at[rows, :], w_sem.at[m, p])

    def ring(me, n, fn):
        def step(k, c):
            fn(lax.rem(me + k, n))
            return c
        lax.fori_loop(1, n, step, 0)

    def other_tensor(fn):
        ring(me_t, nt, fn)

    def other_dp(fn):
        ring(me_d, nd, fn)

    def other_owners(fn):
        if is_owner_all:
            ring(me_d, nd, fn)
        else:
            def step(j, c):
                pl.when(j != me_d)(functools.partial(fn, j))
                return c
            lax.fori_loop(0, owners, step, 0)

    def if_owner(fn):
        if is_owner_all:
            fn()
        else:
            pl.when(me_d < owners)(fn)

    def send(src, dst, s, r, axis, to):
        return pltpu.make_async_remote_copy(
            src_ref=src, dst_ref=dst, send_sem=s, recv_sem=r,
            device_id={axis: to}, device_id_type=MESH)

    for g in range(groups):
        token_copy(g).start()

    barrier = pltpu.get_barrier_semaphore()
    other_tensor(lambda t: pl.semaphore_signal(
        barrier, inc=1, device_id={"tensor": t}, device_id_type=MESH))
    other_dp(lambda d: pl.semaphore_signal(
        barrier, inc=1, device_id={"dp": d}, device_id_type=MESH))

    router_rows = router[...]

    for c in range(CHUNKS):
        def partial_logits(gl, carry, c=c):
            g = c * per + gl
            token_copy(g).wait()
            raw = lax.dot_general(router_rows, tok[g], NT, preferred_element_type=f32)
            rows = pl.ds(pl.multiple_of(gl * 16, 16), 16)
            for q in range(nt):
                stat[c, q, rows, :] = raw[:, q * quarter:(q + 1) * quarter]
                acc = jnp.zeros((quarter, LANES), f32)
                for b in range(owners):
                    part = tok[g, q * quarter:(q + 1) * quarter, b * LANES:(b + 1) * LANES].astype(f32)
                    acc = acc + part * part
                stat[c, q, pl.ds(per * 16 + gl, 1), :] = jnp.sum(acc.T, axis=0, keepdims=True)
            return carry
        stat[c, :, per * 16:, :] = jnp.zeros((nt, 8, LANES), f32)
        lax.fori_loop(0, per, partial_logits, 0)
        if c == 0:
            pl.semaphore_wait(barrier, nt - 1 + nd - 1)
        other_tensor(lambda t, c=c: send(
            stat.at[c, t], stat_in.at[c, me_t], rs_s.at[c, t], rs_r.at[c, me_t], "tensor", t).start())
        if c == 0:
            for p in range(WPARTS):
                weight_copy(0, p).start()
    for m in (1, 2):
        for p in range(WPARTS):
            weight_copy(m, p).start()

    column = lax.broadcasted_iota(jnp.int32, (16, LANES), 1)
    half = LANES // 2
    total_out[me_t] = jnp.zeros(total_out.shape[1:], f32)
    for c in range(CHUNKS):
        stat_in[c, me_t] = stat[c, me_t]
        other_tensor(lambda t, c=c: send(
            stat.at[c, t], stat_in.at[c, t], rs_s.at[c, t], rs_r.at[c, t], "tensor", t).wait_recv())
        total = stat_in[c, 0]
        for t in range(1, nt):
            total = total + stat_in[c, t]
        norm = lax.rsqrt(total[per * 16:] / full_width + epsilon)
        summary = jnp.zeros((16, LANES), f32)
        all_logits = []
        for gl in range(per):
            g = c * per + gl
            logits = total[gl * 16:(gl + 1) * 16] * norm[gl:gl + 1]
            all_logits.append(logits)
            peak = jnp.max(logits, axis=1, keepdims=True)
            powers = jnp.exp(logits - peak)
            csum = jnp.sum(powers, axis=1, keepdims=True)
            wbuf[c, me_t, gl] = (powers * norm[gl:gl + 1]).astype(bf16)
            summary = jnp.where(column == g, peak, jnp.where(column == half + g, csum, summary))
        sbuf[c, me_t] = summary
        other_tensor(lambda t, c=c: send(
            sbuf.at[c, me_t], sbuf.at[c, me_t], as_s.at[c, t], as_r.at[c, me_t], "tensor", t).start())
        other_tensor(lambda t, c=c: send(
            wbuf.at[c, me_t], wbuf.at[c, me_t], ag_s.at[c, t], ag_r.at[c, me_t], "tensor", t).start())
        for gl in range(per):
            g = c * per + gl
            logits = all_logits[gl]
            row_peak = jnp.max(logits, axis=0, keepdims=True)
            row_powers = jnp.exp(logits - row_peak)
            row_sum = jnp.sum(row_powers, axis=0, keepdims=True)
            combine_out[me_t, g] = (row_powers / row_sum).astype(bf16)
            total_out[me_t, g:g + 1, :] = row_peak + jnp.log(row_sum)

    for c in range(CHUNKS):
        other_tensor(lambda t, c=c: send(
            sbuf.at[c, t], sbuf.at[c, t], as_s.at[c, t], as_r.at[c, t], "tensor", t).wait_recv())
        peak = sbuf[c, 0]
        for q in range(1, nt):
            peak = jnp.maximum(peak, sbuf[c, q])
        factor = [jnp.exp(sbuf[c, q] - peak) for q in range(nt)]
        csum = factor[0] * pltpu.roll(sbuf[c, 0], half, 1)
        for q in range(1, nt):
            csum = csum + factor[q] * pltpu.roll(sbuf[c, q], half, 1)
        mine = jnp.logical_and(column >= c * per, column < (c + 1) * per)
        if c == 0:
            stats[me_d, 0] = jnp.where(mine, peak, 0.0)
            stats[me_d, 1] = jnp.where(mine, csum, 1.0)
        else:
            stats[me_d, 0] = jnp.where(mine, peak, stats[me_d, 0])
            stats[me_d, 1] = jnp.where(mine, csum, stats[me_d, 1])
        other_tensor(lambda t, c=c: send(
            wbuf.at[c, t], wbuf.at[c, t], ag_s.at[c, t], ag_r.at[c, t], "tensor", t).wait_recv())
        for gl in range(per):
            g = c * per + gl
            summed = jnp.zeros((16, width), f32)
            for q in range(nt):
                summed = summed + factor[q][:, g:g + 1] * lax.dot_general(
                    wbuf[c, q, gl], tok[g, q * quarter:(q + 1) * quarter, :], NN,
                    preferred_element_type=f32)
            for j in range(owners):
                pbuf[c, j, gl] = summed[:, j * LANES:(j + 1) * LANES].astype(bf16)
        if c == CHUNKS - 1:
            other_owners(lambda j: send(
                stats.at[me_d], stats.at[me_d], st_s.at[j], st_r.at[me_d], "dp", j).start())
        other_owners(lambda j, c=c: send(
            pbuf.at[c, j], rbuf.at[c, me_d], pr_s.at[c, j], pr_r.at[c, me_d], "dp", j).start())

    other_tensor(lambda t: send(
        combine_out.at[me_t], combine_out.at[me_t], cb_s.at[t], cb_r.at[me_t], "tensor", t).start())
    other_tensor(lambda t: send(
        total_out.at[me_t], total_out.at[me_t], tb_s.at[t], tb_r.at[me_t], "tensor", t).start())

    def spread_matrix(rows, cols, flip):
        a = lax.broadcasted_iota(jnp.int32, (rows, cols), 1 if flip else 0)
        b = lax.broadcasted_iota(jnp.int32, (rows, cols), 0 if flip else 1)
        k, q = a // PAD, a % PAD
        source = (q // SLOTS) * 16 + k * SLOTS + q % SLOTS
        hit = jnp.logical_and(q < groups * SLOTS, source == b)
        return jnp.where(hit, 1.0, 0.0).astype(bf16)

    spread = spread_matrix(nt * PAD, groups * 16, False)
    gather = spread_matrix(groups * 16, nt * PAD, True)

    def reduce_slots():
        for c in range(CHUNKS):
            other_dp(lambda d, c=c: send(
                pbuf.at[c, 0], rbuf.at[c, d], pr_s.at[c, 0], pr_r.at[c, d], "dp", d).wait_recv())
            rbuf[c, me_d] = pbuf[c, me_d]
        other_dp(lambda d: send(
            stats.at[d], stats.at[d], st_s.at[0], st_r.at[d], "dp", d).wait_recv())
        peak = stats[0, 0]
        for i in range(1, nd):
            peak = jnp.maximum(peak, stats[i, 0])
        factor = [jnp.exp(stats[i, 0] - peak) for i in range(nd)]
        den = factor[0] * stats[0, 1]
        for i in range(1, nd):
            den = den + factor[i] * stats[i, 1]
        scale = [f / den for f in factor]
        rows = []
        for g in range(groups):
            c, gl = g // per, g % per
            acc = jnp.zeros((16, LANES), f32)
            for i in range(nd):
                acc = acc + scale[i][:, g:g + 1] * rbuf[c, i, gl].astype(f32)
            rows.append(acc.astype(bf16))
        slot_in = jnp.concatenate(rows, axis=0)
        moved = lax.dot_general(spread, slot_in, NN, preferred_element_type=f32).astype(bf16)
        for k in range(nt):
            abuf[k] = moved[k * PAD:(k + 1) * PAD]
        zin[me_t] = abuf[me_t]
        other_tensor(lambda t: send(
            abuf.at[t], zin.at[me_t], az_s.at[t], az_r.at[me_t], "tensor", t).start())
        other_tensor(lambda t: send(
            abuf.at[t], zin.at[t], az_s.at[t], az_r.at[t], "tensor", t).wait_recv())
        xin[me_d] = zin[...]
        other_dp(lambda d: send(
            zin, xin.at[me_d], ax_s.at[d], ax_r.at[me_d], "dp", d).start())
    if_owner(reduce_slots)
    for c in range(CHUNKS):
        other_tensor(lambda t, c=c: send(
            stat.at[c, t], stat_in.at[c, t], rs_s.at[c, t], rs_r.at[c, t], "tensor", t).wait_send())
        other_tensor(lambda t, c=c: send(
            wbuf.at[c, me_t], wbuf.at[c, me_t], ag_s.at[c, t], ag_r.at[c, t], "tensor", t).wait_send())
        other_tensor(lambda t, c=c: send(
            sbuf.at[c, me_t], sbuf.at[c, me_t], as_s.at[c, t], as_r.at[c, t], "tensor", t).wait_send())
        other_owners(lambda j, c=c: send(
            pbuf.at[c, j], rbuf.at[c, j], pr_s.at[c, j], pr_r.at[c, j], "dp", j).wait_send())
    other_owners(lambda j: send(
        stats.at[me_d], stats.at[me_d], st_s.at[j], st_r.at[j], "dp", j).wait_send())
    other_tensor(lambda t: send(
        combine_out.at[me_t], combine_out.at[t], cb_s.at[t], cb_r.at[t], "tensor", t).wait_send())
    other_tensor(lambda t: send(
        total_out.at[me_t], total_out.at[t], tb_s.at[t], tb_r.at[t], "tensor", t).wait_send())
    other_owners(lambda j: send(
        zin, xin.at[j], ax_s.at[0], ax_r.at[j], "dp", j).wait_recv())

    for i in range(owners):
        for t in range(nt):
            x_all[:, t * width + i * LANES:t * width + (i + 1) * LANES] = xin[i, t]

    for m in (0, 1):
        for p in range(WPARTS):
            weight_copy(m, p).wait()
    fc = 256 if hidden_here % 256 == 0 else hidden_here

    for f in range(hidden_here // fc):
        x = x_all[...]
        gate = lax.dot_general(x, wg[f * fc:(f + 1) * fc, :], NT, preferred_element_type=f32)
        up = lax.dot_general(x, wu[f * fc:(f + 1) * fc, :], NT, preferred_element_type=f32)
        act = gate / (1.0 + jnp.exp(-gate)) * up
        hidden[:, f * fc:(f + 1) * fc] = act.astype(bf16)

    for p in range(WPARTS):
        weight_copy(2, p).wait()

    pairs = owners // 2

    def down_part(k, carry):
        p = lax.rem(k + me_d // 2 + 1, pairs)
        for t in range(nt):
            cols = pl.ds(pl.multiple_of(t * width + p * 2 * LANES, 2 * LANES), 2 * LANES)
            out = lax.dot_general(hidden[...], wd[:, cols], NN, preferred_element_type=f32)
            obuf[2 * p, t] = out[:, :LANES].astype(bf16)
            obuf[2 * p + 1, t] = out[:, LANES:].astype(bf16)
        for h in range(2):
            j = 2 * p + h

            @pl.when(j != me_d)
            def _():
                send(obuf.at[j], oin.at[me_d], or_s.at[j], or_r.at[me_d], "dp", j).start()
        return carry
    lax.fori_loop(0, pairs, down_part, 0)

    def drain_inputs():
        other_tensor(lambda t: send(
            abuf.at[t], zin.at[t], az_s.at[t], az_r.at[t], "tensor", t).wait_send())
        other_dp(lambda d: send(
            zin, xin.at[0], ax_s.at[d], ax_r.at[d], "dp", d).wait_send())
    if_owner(drain_inputs)
    other_tensor(lambda t: send(
        combine_out.at[t], combine_out.at[t], cb_s.at[t], cb_r.at[t], "tensor", t).wait_recv())
    other_tensor(lambda t: send(
        total_out.at[t], total_out.at[t], tb_s.at[t], tb_r.at[t], "tensor", t).wait_recv())

    def reduce_outputs():
        oin[me_d] = obuf[me_d]
        other_dp(lambda d: send(
            obuf.at[0], oin.at[d], or_s.at[0], or_r.at[d], "dp", d).wait_recv())
        for t in range(nt):
            acc = oin[0, t].astype(f32)
            for i in range(1, nd):
                acc = acc + oin[i, t].astype(f32)
            bbuf[t] = acc.astype(bf16)
        zout[me_t] = bbuf[me_t]
        other_tensor(lambda t: send(
            bbuf.at[t], zout.at[me_t], bz_s.at[t], bz_r.at[me_t], "tensor", t).start())
        other_tensor(lambda t: send(
            bbuf.at[t], zout.at[t], bz_s.at[t], bz_r.at[t], "tensor", t).wait_recv())
        rows = jnp.concatenate([zout[k] for k in range(nt)], axis=0)
        window_out[me_d] = lax.dot_general(
            gather, rows, NN, preferred_element_type=f32).astype(bf16)
        other_dp(lambda d: send(
            window_out.at[me_d], window_out.at[me_d], bx_s.at[d], bx_r.at[me_d], "dp", d).start())
    if_owner(reduce_outputs)
    other_owners(lambda j: send(
        window_out.at[j], window_out.at[j], bx_s.at[0], bx_r.at[j], "dp", j).wait_recv())

    other_owners(lambda j: send(
        obuf.at[j], oin.at[j], or_s.at[j], or_r.at[j], "dp", j).wait_send())

    def drain():
        other_tensor(lambda t: send(
            bbuf.at[t], zout.at[t], bz_s.at[t], bz_r.at[t], "tensor", t).wait_send())
        other_dp(lambda d: send(
            window_out.at[me_d], window_out.at[me_d], bx_s.at[d], bx_r.at[d], "dp", d).wait_send())
    if_owner(drain)


def mix_kernel(combine, window, total, mixed, total_out, held, sem):
    nt, groups = combine.shape[:2]
    owners, quarter = window.shape[0], combine.shape[3]

    def copy(g):
        return pltpu.make_async_copy(held.at[g], mixed.at[g], sem.at[g])

    for g in range(groups):
        slots = jnp.concatenate([window[j, g] for j in range(owners)], axis=1)
        for q in range(nt):
            held[g, q * quarter:(q + 1) * quarter, :] = lax.dot_general(
                combine[q, g], slots, (((0,), (0,)), ((), ())),
                preferred_element_type=f32).astype(bf16)
        copy(g).start()
    for q in range(nt):
        total_out[:, q * quarter:(q + 1) * quarter] = total[q, :groups, :]
    for g in range(groups):
        copy(g).wait()


def per_device(tokens, router, w_gate, w_up, w_down):
    nd, nt = lax.axis_size("dp"), lax.axis_size("tensor")
    groups, count, width = tokens.shape
    hidden_here, full = w_gate.shape[1:]
    slots = router.shape[0]
    owners = width // LANES
    quarter = count // nt
    per = groups // CHUNKS
    srows = per * 16 + 8
    VM, DMA = pltpu.VMEM, pltpu.SemaphoreType.DMA
    any_spec = pl.BlockSpec(memory_space=pl.ANY)
    vmem_spec = pl.BlockSpec(memory_space=pltpu.VMEM)
    window, combine, total = pl.pallas_call(
        functools.partial(dispatch_kernel, nd, nt),
        out_shape=(
            jax.ShapeDtypeStruct((owners, groups * slots, LANES), bf16),
            jax.ShapeDtypeStruct((nt, groups, slots, quarter), bf16),
            jax.ShapeDtypeStruct((nt, 8, quarter), f32),
        ),
        in_specs=[any_spec, vmem_spec, any_spec, any_spec, any_spec],
        out_specs=(vmem_spec, vmem_spec, vmem_spec),
        scratch_shapes=[
            VM((groups, count, width), bf16),
            VM((hidden_here, full), bf16),
            VM((hidden_here, full), bf16),
            VM((hidden_here, full), bf16),
            VM((CHUNKS, nt, srows, quarter), f32),
            VM((CHUNKS, nt, srows, quarter), f32),
            VM((CHUNKS, nt, per, slots, quarter), bf16),
            VM((CHUNKS, nt, slots, LANES), f32),
            VM((nd, 2, slots, LANES), f32),
            VM((CHUNKS, owners, per, slots, LANES), bf16),
            VM((CHUNKS, nd, per, slots, LANES), bf16),
            VM((nt, PAD, LANES), bf16),
            VM((nt, PAD, LANES), bf16),
            VM((owners, nt, PAD, LANES), bf16),
            VM((PAD, full), bf16),
            VM((PAD, hidden_here), bf16),
            VM((owners, nt, PAD, LANES), bf16),
            VM((nd, nt, PAD, LANES), bf16),
            VM((nt, PAD, LANES), bf16),
            VM((nt, PAD, LANES), bf16),
            DMA((groups,)), DMA((3, WPARTS)),
            DMA((CHUNKS, nt)), DMA((CHUNKS, nt)), DMA((CHUNKS, nt)), DMA((CHUNKS, nt)),
            DMA((CHUNKS, nt)), DMA((CHUNKS, nt)), DMA((nt,)), DMA((nt,)), DMA((nt,)), DMA((nt,)),
            DMA((owners,)), DMA((nd,)), DMA((CHUNKS, owners)), DMA((CHUNKS, nd)),
            DMA((nt,)), DMA((nt,)), DMA((nd,)), DMA((owners,)),
            DMA((owners,)), DMA((nd,)), DMA((nt,)), DMA((nt,)), DMA((nd,)), DMA((owners,)),
        ],
        compiler_params=pltpu.CompilerParams(
            collective_id=0, has_side_effects=True, vmem_limit_bytes=58 * 1024 * 1024),
        name="dispatch",
    )(tokens, router, w_gate[0], w_up[0], w_down[0])
    window = window.reshape(owners, groups, slots, LANES)
    mixed, log_total = pl.pallas_call(
        mix_kernel,
        out_shape=(
            jax.ShapeDtypeStruct((groups, count, width), bf16),
            jax.ShapeDtypeStruct((groups, count), f32),
        ),
        in_specs=[vmem_spec, vmem_spec, vmem_spec],
        out_specs=(any_spec, vmem_spec),
        scratch_shapes=[VM((groups, count, width), bf16), DMA((groups,))],
        compiler_params=pltpu.CompilerParams(vmem_limit_bytes=32 * 1024 * 1024),
        name="mix",
    )(combine, window, total)
    return (mixed, log_total)


def solution(mesh):
    in_specs = (
        P(None, "dp", "tensor"),
        P(None, "tensor"),
        P("tensor", "dp", None),
        P("tensor", "dp", None),
        P("tensor", "dp", None),
    )
    out_specs = (P(None, "dp", "tensor"), P(None, "dp"))
    return jax.shard_map(
        per_device, mesh=mesh, in_specs=in_specs, out_specs=out_specs, check_vma=False
    )
```

```python
import functools

import jax
import jax.numpy as jnp
from jax import lax
from jax.experimental import pallas as pl
from jax.experimental.pallas import tpu as pltpu
from jax.sharding import PartitionSpec as P

SLOTS = 4
ROWS = 16
LANES = 128
CHUNKS = 2
PAD = ROWS * CHUNKS
WPARTS = 4
epsilon = 1e-05
f32 = jnp.float32
bf16 = jnp.bfloat16
MESH = pl.DeviceIdType.MESH
NT = (((1,), (1,)), ((), ()))
NN = (((1,), (0,)), ((), ()))


def dispatch_kernel(
    nd, nt, tokens, router, w_gate, w_up, w_down,
    window_out, combine_out, total_out,
    tok, wg, wu, wd, stat, stat_in, wbuf, sbuf, stats, pbuf, rbuf, abuf, zin, xin, gate_acc, up_acc, hidden,
    obuf, oin, bbuf, zout, combine, total_log, mine_out,
    tok_sem, w_sem, out_sem,
    rs_s, rs_r, ag_s, ag_r, as_s, as_r, cb_s, cb_r, tb_s, tb_r, st_s, st_r, pr_s, pr_r, az_s, az_r, ax_s, ax_r,
    or_s, or_r, bz_s, bz_r, bx_s, bx_r,
):
    me_d, me_t = lax.axis_index("dp"), lax.axis_index("tensor")
    groups, count, width = tok.shape
    owners = width // LANES
    quarter = count // nt
    per = groups // CHUNKS
    full_width = width * nt
    hidden_here = wg.shape[0]
    wrows = hidden_here // WPARTS
    is_owner_all = nd == owners

    def token_copy(g):
        return pltpu.make_async_copy(tokens.at[g], tok.at[g], tok_sem.at[g])

    def weight_copy(m, p):
        src, dst = ((w_gate, wg), (w_up, wu), (w_down, wd))[m]
        rows = pl.ds(p * wrows, wrows)
        return pltpu.make_async_copy(src.at[rows, :], dst.at[rows, :], w_sem.at[m, p])

    def ring(me, n, fn):
        def step(k, c):
            fn(lax.rem(me + k, n))
            return c
        lax.fori_loop(1, n, step, 0)

    def other_tensor(fn):
        ring(me_t, nt, fn)

    def other_dp(fn):
        ring(me_d, nd, fn)

    def other_owners(fn):
        if is_owner_all:
            ring(me_d, nd, fn)
        else:
            def step(j, c):
                pl.when(j != me_d)(functools.partial(fn, j))
                return c
            lax.fori_loop(0, owners, step, 0)

    def if_owner(fn):
        if is_owner_all:
            fn()
        else:
            pl.when(me_d < owners)(fn)

    def send(src, dst, s, r, axis, to):
        return pltpu.make_async_remote_copy(
            src_ref=src, dst_ref=dst, send_sem=s, recv_sem=r,
            device_id={axis: to}, device_id_type=MESH)

    for g in range(groups):
        token_copy(g).start()

    barrier = pltpu.get_barrier_semaphore()
    other_tensor(lambda t: pl.semaphore_signal(
        barrier, inc=1, device_id={"tensor": t}, device_id_type=MESH))
    other_dp(lambda d: pl.semaphore_signal(
        barrier, inc=1, device_id={"dp": d}, device_id_type=MESH))

    router_rows = router[...]

    for c in range(CHUNKS):
        def partial_logits(gl, carry, c=c):
            g = c * per + gl
            token_copy(g).wait()
            raw = lax.dot_general(router_rows, tok[g], NT, preferred_element_type=f32)
            rows = pl.ds(pl.multiple_of(gl * 16, 16), 16)
            for q in range(nt):
                stat[c, q, rows, :] = raw[:, q * quarter:(q + 1) * quarter]
                acc = jnp.zeros((quarter, LANES), f32)
                for b in range(owners):
                    part = tok[g, q * quarter:(q + 1) * quarter, b * LANES:(b + 1) * LANES].astype(f32)
                    acc = acc + part * part
                stat[c, q, pl.ds(per * 16 + gl, 1), :] = jnp.sum(acc.T, axis=0, keepdims=True)
            return carry
        stat[c, :, per * 16:, :] = jnp.zeros((nt, 8, LANES), f32)
        lax.fori_loop(0, per, partial_logits, 0)
        if c == 0:
            pl.semaphore_wait(barrier, nt - 1 + nd - 1)
        other_tensor(lambda t, c=c: send(
            stat.at[c, t], stat_in.at[c, me_t], rs_s.at[c, t], rs_r.at[c, me_t], "tensor", t).start())
        if c == 0:
            for p in range(WPARTS):
                weight_copy(0, p).start()
    for m in (1, 2):
        for p in range(WPARTS):
            weight_copy(m, p).start()

    column = lax.broadcasted_iota(jnp.int32, (16, LANES), 1)
    half = LANES // 2
    total_log[me_t] = jnp.zeros(total_log.shape[1:], f32)
    for c in range(CHUNKS):
        stat_in[c, me_t] = stat[c, me_t]
        other_tensor(lambda t, c=c: send(
            stat.at[c, t], stat_in.at[c, t], rs_s.at[c, t], rs_r.at[c, t], "tensor", t).wait_recv())
        total = stat_in[c, 0]
        for t in range(1, nt):
            total = total + stat_in[c, t]
        norm = lax.rsqrt(total[per * 16:] / full_width + epsilon)
        summary = jnp.zeros((16, LANES), f32)
        all_logits = []
        for gl in range(per):
            g = c * per + gl
            logits = total[gl * 16:(gl + 1) * 16] * norm[gl:gl + 1]
            all_logits.append(logits)
            peak = jnp.max(logits, axis=1, keepdims=True)
            powers = jnp.exp(logits - peak)
            csum = jnp.sum(powers, axis=1, keepdims=True)
            wbuf[c, me_t, gl] = (powers * norm[gl:gl + 1]).astype(bf16)
            summary = jnp.where(column == g, peak, jnp.where(column == half + g, csum, summary))
        sbuf[c, me_t] = summary
        other_tensor(lambda t, c=c: send(
            sbuf.at[c, me_t], sbuf.at[c, me_t], as_s.at[c, t], as_r.at[c, me_t], "tensor", t).start())
        other_tensor(lambda t, c=c: send(
            wbuf.at[c, me_t], wbuf.at[c, me_t], ag_s.at[c, t], ag_r.at[c, me_t], "tensor", t).start())
        for gl in range(per):
            g = c * per + gl
            logits = all_logits[gl]
            row_peak = jnp.max(logits, axis=0, keepdims=True)
            row_powers = jnp.exp(logits - row_peak)
            row_sum = jnp.sum(row_powers, axis=0, keepdims=True)
            combine[me_t, g] = (row_powers / row_sum).astype(bf16)
            total_log[me_t, g:g + 1, :] = row_peak + jnp.log(row_sum)

    for c in range(CHUNKS):
        other_tensor(lambda t, c=c: send(
            sbuf.at[c, t], sbuf.at[c, t], as_s.at[c, t], as_r.at[c, t], "tensor", t).wait_recv())
        peak = sbuf[c, 0]
        for q in range(1, nt):
            peak = jnp.maximum(peak, sbuf[c, q])
        factor = [jnp.exp(sbuf[c, q] - peak) for q in range(nt)]
        csum = factor[0] * pltpu.roll(sbuf[c, 0], half, 1)
        for q in range(1, nt):
            csum = csum + factor[q] * pltpu.roll(sbuf[c, q], half, 1)
        mine = jnp.logical_and(column >= c * per, column < (c + 1) * per)
        stats[c, me_d, 0] = jnp.where(mine, peak, 0.0)
        stats[c, me_d, 1] = jnp.where(mine, csum, 1.0)
        other_tensor(lambda t, c=c: send(
            wbuf.at[c, t], wbuf.at[c, t], ag_s.at[c, t], ag_r.at[c, t], "tensor", t).wait_recv())
        for gl in range(per):
            g = c * per + gl
            summed = jnp.zeros((16, width), f32)
            for q in range(nt):
                summed = summed + factor[q][:, g:g + 1] * lax.dot_general(
                    wbuf[c, q, gl], tok[g, q * quarter:(q + 1) * quarter, :], NN,
                    preferred_element_type=f32)
            for j in range(owners):
                pbuf[c, j, gl] = summed[:, j * LANES:(j + 1) * LANES].astype(bf16)
        other_owners(lambda j, c=c: send(
            stats.at[c, me_d], stats.at[c, me_d], st_s.at[c, j], st_r.at[c, me_d], "dp", j).start())
        other_owners(lambda j, c=c: send(
            pbuf.at[c, j], rbuf.at[c, me_d], pr_s.at[c, j], pr_r.at[c, me_d], "dp", j).start())

    other_tensor(lambda t: send(
        combine.at[me_t], combine.at[me_t], cb_s.at[t], cb_r.at[me_t], "tensor", t).start())
    other_tensor(lambda t: send(
        total_log.at[me_t], total_log.at[me_t], tb_s.at[t], tb_r.at[me_t], "tensor", t).start())

    def spread_matrix(chunks, flip):
        shape = (nt * chunks * ROWS, chunks * per * 16)
        a = lax.broadcasted_iota(jnp.int32, shape[::-1] if flip else shape, 1 if flip else 0)
        b = lax.broadcasted_iota(jnp.int32, shape[::-1] if flip else shape, 0 if flip else 1)
        k, c, q = a // (chunks * ROWS), (a // ROWS) % chunks, a % ROWS
        source = (c * per + q // SLOTS) * 16 + k * SLOTS + q % SLOTS
        hit = jnp.logical_and(q < per * SLOTS, source == b)
        return jnp.where(hit, 1.0, 0.0).astype(bf16)

    spread = spread_matrix(1, False)
    gather = spread_matrix(CHUNKS, True)

    def reduce_slots():
        for c in range(CHUNKS):
            other_dp(lambda d, c=c: send(
                stats.at[c, d], stats.at[c, d], st_s.at[c, 0], st_r.at[c, d], "dp", d).wait_recv())
            peak = stats[c, 0, 0]
            for i in range(1, nd):
                peak = jnp.maximum(peak, stats[c, i, 0])
            factor = [jnp.exp(stats[c, i, 0] - peak) for i in range(nd)]
            den = factor[0] * stats[c, 0, 1]
            for i in range(1, nd):
                den = den + factor[i] * stats[c, i, 1]
            scale = [f / den for f in factor]
            other_dp(lambda d, c=c: send(
                pbuf.at[c, 0], rbuf.at[c, d], pr_s.at[c, 0], pr_r.at[c, d], "dp", d).wait_recv())
            rbuf[c, me_d] = pbuf[c, me_d]
            rows = []
            for gl in range(per):
                g = c * per + gl
                acc = jnp.zeros((16, LANES), f32)
                for i in range(nd):
                    acc = acc + scale[i][:, g:g + 1] * rbuf[c, i, gl].astype(f32)
                rows.append(acc.astype(bf16))
            slot_in = jnp.concatenate(rows, axis=0)
            moved = lax.dot_general(spread, slot_in, NN, preferred_element_type=f32).astype(bf16)
            for k in range(nt):
                abuf[c, k] = moved[k * ROWS:(k + 1) * ROWS]
            zin[c, me_t] = abuf[c, me_t]
            other_tensor(lambda t, c=c: send(
                abuf.at[c, t], zin.at[c, me_t], az_s.at[c, t], az_r.at[c, me_t], "tensor", t).start())
            other_tensor(lambda t, c=c: send(
                abuf.at[c, t], zin.at[c, t], az_s.at[c, t], az_r.at[c, t], "tensor", t).wait_recv())
            xin[me_d, c] = zin[c]
            other_dp(lambda d, c=c: send(
                zin.at[c], xin.at[me_d, c], ax_s.at[c, d], ax_r.at[c, me_d], "dp", d).start())
    if_owner(reduce_slots)
    for c in range(CHUNKS):
        other_tensor(lambda t, c=c: send(
            stat.at[c, t], stat_in.at[c, t], rs_s.at[c, t], rs_r.at[c, t], "tensor", t).wait_send())
        other_tensor(lambda t, c=c: send(
            wbuf.at[c, me_t], wbuf.at[c, me_t], ag_s.at[c, t], ag_r.at[c, t], "tensor", t).wait_send())
        other_tensor(lambda t, c=c: send(
            sbuf.at[c, me_t], sbuf.at[c, me_t], as_s.at[c, t], as_r.at[c, t], "tensor", t).wait_send())
        other_owners(lambda j, c=c: send(
            pbuf.at[c, j], rbuf.at[c, j], pr_s.at[c, j], pr_r.at[c, j], "dp", j).wait_send())
        other_owners(lambda j, c=c: send(
            stats.at[c, me_d], stats.at[c, me_d], st_s.at[c, j], st_r.at[c, j], "dp", j).wait_send())
    other_tensor(lambda t: send(
        combine.at[me_t], combine.at[t], cb_s.at[t], cb_r.at[t], "tensor", t).wait_send())
    other_tensor(lambda t: send(
        total_log.at[me_t], total_log.at[t], tb_s.at[t], tb_r.at[t], "tensor", t).wait_send())
    for m in (0, 1):
        for p in range(WPARTS):
            weight_copy(m, p).wait()
    pairs = owners // 2
    fc = 256 if hidden_here % 256 == 0 else hidden_here
    gate_acc[...] = jnp.zeros(gate_acc.shape, f32)
    up_acc[...] = jnp.zeros(up_acc.shape, f32)

    def feature_part(k, carry):
        p = lax.rem(k + me_d // 2, pairs)
        for h in range(2):
            j = 2 * p + h

            @pl.when(j != me_d)
            def _():
                for c in range(CHUNKS):
                    send(zin.at[c], xin.at[j, c], ax_s.at[c, 0], ax_r.at[c, j], "dp", j).wait_recv()
        xs = []
        for t in range(nt):
            xs.append(jnp.concatenate([
                jnp.concatenate([xin[2 * p + h, c, t] for c in range(CHUNKS)], axis=0)
                for h in range(2)], axis=1))
        for f in range(hidden_here // fc):
            rows = slice(f * fc, (f + 1) * fc)
            for w, acc in ((wg, gate_acc), (wu, up_acc)):
                part = acc[:, rows]
                for t in range(nt):
                    cols = pl.ds(pl.multiple_of(t * width + p * 2 * LANES, 2 * LANES), 2 * LANES)
                    part = part + lax.dot_general(xs[t], w[rows, cols], NT, preferred_element_type=f32)
                acc[:, rows] = part
        return carry
    lax.fori_loop(0, pairs, feature_part, 0)
    gate = gate_acc[...]
    hidden[...] = (gate / (1.0 + jnp.exp(-gate)) * up_acc[...]).astype(bf16)

    for p in range(WPARTS):
        weight_copy(2, p).wait()

    def down_part(k, carry):
        p = lax.rem(k + me_d // 2 + 1, pairs)
        for t in range(nt):
            cols = pl.ds(pl.multiple_of(t * width + p * 2 * LANES, 2 * LANES), 2 * LANES)
            out = lax.dot_general(hidden[...], wd[:, cols], NN, preferred_element_type=f32)
            obuf[2 * p, t] = out[:, :LANES].astype(bf16)
            obuf[2 * p + 1, t] = out[:, LANES:].astype(bf16)
        for h in range(2):
            j = 2 * p + h

            @pl.when(j != me_d)
            def _():
                send(obuf.at[j], oin.at[me_d], or_s.at[j], or_r.at[me_d], "dp", j).start()
        return carry
    lax.fori_loop(0, pairs, down_part, 0)

    def drain_inputs():
        for c in range(CHUNKS):
            other_tensor(lambda t, c=c: send(
                abuf.at[c, t], zin.at[c, t], az_s.at[c, t], az_r.at[c, t], "tensor", t).wait_send())
            other_dp(lambda d, c=c: send(
                zin.at[c], xin.at[0, c], ax_s.at[c, d], ax_r.at[c, d], "dp", d).wait_send())
    if_owner(drain_inputs)
    other_tensor(lambda t: send(
        combine.at[t], combine.at[t], cb_s.at[t], cb_r.at[t], "tensor", t).wait_recv())
    other_tensor(lambda t: send(
        total_log.at[t], total_log.at[t], tb_s.at[t], tb_r.at[t], "tensor", t).wait_recv())
    combine_write = pltpu.make_async_copy(combine, combine_out, out_sem.at[0])
    total_write = pltpu.make_async_copy(total_log, total_out, out_sem.at[1])
    combine_write.start()
    total_write.start()

    def reduce_outputs():
        oin[me_d] = obuf[me_d]
        other_dp(lambda d: send(
            obuf.at[0], oin.at[d], or_s.at[0], or_r.at[d], "dp", d).wait_recv())
        for t in range(nt):
            acc = oin[0, t].astype(f32)
            for i in range(1, nd):
                acc = acc + oin[i, t].astype(f32)
            bbuf[t] = acc.astype(bf16)
        zout[me_t] = bbuf[me_t]
        other_tensor(lambda t: send(
            bbuf.at[t], zout.at[me_t], bz_s.at[t], bz_r.at[me_t], "tensor", t).start())
        other_tensor(lambda t: send(
            bbuf.at[t], zout.at[t], bz_s.at[t], bz_r.at[t], "tensor", t).wait_recv())
        rows = jnp.concatenate([zout[k] for k in range(nt)], axis=0)
        mine_out[...] = lax.dot_general(
            gather, rows, NN, preferred_element_type=f32).astype(bf16)
        other_dp(lambda d: send(
            mine_out, window_out.at[me_d], bx_s.at[d], bx_r.at[me_d], "dp", d).start())
        pltpu.make_async_copy(mine_out, window_out.at[me_d], out_sem.at[2]).start()
    if_owner(reduce_outputs)
    other_owners(lambda j: send(
        mine_out, window_out.at[j], bx_s.at[0], bx_r.at[j], "dp", j).wait_recv())

    other_owners(lambda j: send(
        obuf.at[j], oin.at[j], or_s.at[j], or_r.at[j], "dp", j).wait_send())

    def drain():
        other_tensor(lambda t: send(
            bbuf.at[t], zout.at[t], bz_s.at[t], bz_r.at[t], "tensor", t).wait_send())
        other_dp(lambda d: send(
            mine_out, window_out.at[me_d], bx_s.at[d], bx_r.at[d], "dp", d).wait_send())
        pltpu.make_async_copy(mine_out, window_out.at[me_d], out_sem.at[2]).wait()
    if_owner(drain)
    combine_write.wait()
    total_write.wait()


def mix_kernel(combine_in, window_in, total_in, mixed, total_out, combine, window, total, held, in_sem, sem):
    loads = [
        pltpu.make_async_copy(combine_in, combine, in_sem.at[0]),
        pltpu.make_async_copy(window_in, window, in_sem.at[1]),
        pltpu.make_async_copy(total_in, total, in_sem.at[2]),
    ]
    for load in loads:
        load.start()
    nt, groups = combine.shape[:2]
    owners, quarter = window.shape[0], combine.shape[3]

    def copy(g):
        return pltpu.make_async_copy(held.at[g], mixed.at[g], sem.at[g])

    for load in loads:
        load.wait()
    for g in range(groups):
        slots = jnp.concatenate([window[j, g] for j in range(owners)], axis=1)
        for q in range(nt):
            held[g, q * quarter:(q + 1) * quarter, :] = lax.dot_general(
                combine[q, g], slots, (((0,), (0,)), ((), ())),
                preferred_element_type=f32).astype(bf16)
        copy(g).start()
    for q in range(nt):
        total_out[:, q * quarter:(q + 1) * quarter] = total[q, :groups, :]
    for g in range(groups):
        copy(g).wait()


def per_device(tokens, router, w_gate, w_up, w_down):
    nd, nt = lax.axis_size("dp"), lax.axis_size("tensor")
    groups, count, width = tokens.shape
    hidden_here, full = w_gate.shape[1:]
    slots = router.shape[0]
    owners = width // LANES
    quarter = count // nt
    per = groups // CHUNKS
    srows = per * 16 + 8
    VM, DMA = pltpu.VMEM, pltpu.SemaphoreType.DMA
    any_spec = pl.BlockSpec(memory_space=pl.ANY)
    vmem_spec = pl.BlockSpec(memory_space=pltpu.VMEM)
    hbm_spec = pl.BlockSpec(memory_space=pltpu.HBM)
    window, combine, total = pl.pallas_call(
        functools.partial(dispatch_kernel, nd, nt),
        out_shape=(
            jax.ShapeDtypeStruct((owners, groups * slots, LANES), bf16),
            jax.ShapeDtypeStruct((nt, groups, slots, quarter), bf16),
            jax.ShapeDtypeStruct((nt, 8, quarter), f32),
        ),
        in_specs=[any_spec, vmem_spec, any_spec, any_spec, any_spec],
        out_specs=(hbm_spec, hbm_spec, hbm_spec),
        scratch_shapes=[
            VM((groups, count, width), bf16),
            VM((hidden_here, full), bf16),
            VM((hidden_here, full), bf16),
            VM((hidden_here, full), bf16),
            VM((CHUNKS, nt, srows, quarter), f32),
            VM((CHUNKS, nt, srows, quarter), f32),
            VM((CHUNKS, nt, per, slots, quarter), bf16),
            VM((CHUNKS, nt, slots, LANES), f32),
            VM((CHUNKS, nd, 2, slots, LANES), f32),
            VM((CHUNKS, owners, per, slots, LANES), bf16),
            VM((CHUNKS, nd, per, slots, LANES), bf16),
            VM((CHUNKS, nt, ROWS, LANES), bf16),
            VM((CHUNKS, nt, ROWS, LANES), bf16),
            VM((owners, CHUNKS, nt, ROWS, LANES), bf16),
            VM((PAD, hidden_here), f32),
            VM((PAD, hidden_here), f32),
            VM((PAD, hidden_here), bf16),
            VM((owners, nt, PAD, LANES), bf16),
            VM((nd, nt, PAD, LANES), bf16),
            VM((nt, PAD, LANES), bf16),
            VM((nt, PAD, LANES), bf16),
            VM((nt, groups, slots, quarter), bf16),
            VM((nt, 8, quarter), f32),
            VM((groups * slots, LANES), bf16),
            DMA((groups,)), DMA((3, WPARTS)), DMA((3,)),
            DMA((CHUNKS, nt)), DMA((CHUNKS, nt)), DMA((CHUNKS, nt)), DMA((CHUNKS, nt)),
            DMA((CHUNKS, nt)), DMA((CHUNKS, nt)), DMA((nt,)), DMA((nt,)), DMA((nt,)), DMA((nt,)),
            DMA((CHUNKS, owners)), DMA((CHUNKS, nd)), DMA((CHUNKS, owners)), DMA((CHUNKS, nd)),
            DMA((CHUNKS, nt)), DMA((CHUNKS, nt)), DMA((CHUNKS, nd)), DMA((CHUNKS, owners)),
            DMA((owners,)), DMA((nd,)), DMA((nt,)), DMA((nt,)), DMA((nd,)), DMA((owners,)),
        ],
        compiler_params=pltpu.CompilerParams(
            collective_id=0, has_side_effects=True, vmem_limit_bytes=58 * 1024 * 1024),
        name="dispatch",
    )(tokens, router, w_gate[0], w_up[0], w_down[0])
    window = window.reshape(owners, groups, slots, LANES)
    mixed, log_total = pl.pallas_call(
        mix_kernel,
        out_shape=(
            jax.ShapeDtypeStruct((groups, count, width), bf16),
            jax.ShapeDtypeStruct((groups, count), f32),
        ),
        in_specs=[hbm_spec, hbm_spec, hbm_spec],
        out_specs=(any_spec, vmem_spec),
        scratch_shapes=[
            VM(combine.shape, bf16), VM(window.shape, bf16), VM(total.shape, f32),
            VM((groups, count, width), bf16), DMA((3,)), DMA((groups,)),
        ],
        compiler_params=pltpu.CompilerParams(vmem_limit_bytes=60 * 1024 * 1024),
        name="mix",
    )(combine, window, total)
    return (mixed, log_total)


def solution(mesh):
    in_specs = (
        P(None, "dp", "tensor"),
        P(None, "tensor"),
        P("tensor", "dp", None),
        P("tensor", "dp", None),
        P("tensor", "dp", None),
    )
    out_specs = (P(None, "dp", "tensor"), P(None, "dp"))
    return jax.shard_map(
        per_device, mesh=mesh, in_specs=in_specs, out_specs=out_specs, check_vma=False
    )
```

```python
import functools

import jax
import jax.numpy as jnp
from jax import lax
from jax.experimental import pallas as pl
from jax.experimental.pallas import tpu as pltpu
from jax.sharding import PartitionSpec as P

SLOTS = 4
ROWS = 16
LANES = 128
CHUNKS = 2
PAD = ROWS * CHUNKS
WPARTS = 4
epsilon = 1e-05
f32 = jnp.float32
bf16 = jnp.bfloat16
MESH = pl.DeviceIdType.MESH
NT = (((1,), (1,)), ((), ()))
NN = (((1,), (0,)), ((), ()))


def dispatch_kernel(
    nd, nt, tokens, router, w_gate, w_up, w_down,
    window_out, combine_out, total_out,
    tok, wg, wu, wd, stat, stat_in, wbuf, sbuf, stats, pbuf, rbuf, abuf, zin, xin, gate_acc, up_acc, hidden,
    obuf, oin, bbuf, zout, combine, total_log, mine_out,
    tok_sem, w_sem, out_sem,
    rs_s, rs_r, ag_s, ag_r, as_s, as_r, cb_s, cb_r, tb_s, tb_r, st_s, st_r, pr_s, pr_r, az_s, az_r, ax_s, ax_r,
    or_s, or_r, bz_s, bz_r, bx_s, bx_r,
):
    me_d, me_t = lax.axis_index("dp"), lax.axis_index("tensor")
    groups, count, width = tok.shape
    owners = width // LANES
    quarter = count // nt
    per = groups // CHUNKS
    full_width = width * nt
    hidden_here = wg.shape[0]
    wrows = hidden_here // WPARTS
    is_owner_all = nd == owners

    def token_copy(g):
        return pltpu.make_async_copy(tokens.at[g], tok.at[g], tok_sem.at[g])

    def weight_copy(m, p):
        src, dst = ((w_gate, wg), (w_up, wu), (w_down, wd))[m]
        rows = pl.ds(p * wrows, wrows)
        return pltpu.make_async_copy(src.at[rows, :], dst.at[rows, :], w_sem.at[m, p])

    def ring(me, n, fn):
        def step(k, c):
            fn(lax.rem(me + k, n))
            return c
        lax.fori_loop(1, n, step, 0)

    def other_tensor(fn):
        ring(me_t, nt, fn)

    def other_dp(fn):
        ring(me_d, nd, fn)

    def other_owners(fn):
        if is_owner_all:
            ring(me_d, nd, fn)
        else:
            def step(j, c):
                pl.when(j != me_d)(functools.partial(fn, j))
                return c
            lax.fori_loop(0, owners, step, 0)

    def if_owner(fn):
        if is_owner_all:
            fn()
        else:
            pl.when(me_d < owners)(fn)

    def send(src, dst, s, r, axis, to):
        return pltpu.make_async_remote_copy(
            src_ref=src, dst_ref=dst, send_sem=s, recv_sem=r,
            device_id={axis: to}, device_id_type=MESH)

    for g in range(groups):
        token_copy(g).start()
    for m in range(3):
        for p in range(WPARTS):
            weight_copy(m, p).start()

    barrier = pltpu.get_barrier_semaphore()
    other_tensor(lambda t: pl.semaphore_signal(
        barrier, inc=1, device_id={"tensor": t}, device_id_type=MESH))
    other_dp(lambda d: pl.semaphore_signal(
        barrier, inc=1, device_id={"dp": d}, device_id_type=MESH))

    router_rows = router[...]

    for c in range(CHUNKS):
        def partial_logits(gl, carry, c=c):
            g = c * per + gl
            token_copy(g).wait()
            raw = lax.dot_general(router_rows, tok[g], NT, preferred_element_type=f32)
            rows = pl.ds(pl.multiple_of(gl * 16, 16), 16)
            for q in range(nt):
                stat[c, q, rows, :] = raw[:, q * quarter:(q + 1) * quarter]
                acc = jnp.zeros((quarter, LANES), f32)
                for b in range(owners):
                    part = tok[g, q * quarter:(q + 1) * quarter, b * LANES:(b + 1) * LANES].astype(f32)
                    acc = acc + part * part
                stat[c, q, pl.ds(per * 16 + gl, 1), :] = jnp.sum(acc.T, axis=0, keepdims=True)
            return carry
        stat[c, :, per * 16:, :] = jnp.zeros((nt, 8, LANES), f32)
        lax.fori_loop(0, per, partial_logits, 0)
        if c == 0:
            pl.semaphore_wait(barrier, nt - 1 + nd - 1)
        other_tensor(lambda t, c=c: send(
            stat.at[c, t], stat_in.at[c, me_t], rs_s.at[c, t], rs_r.at[c, me_t], "tensor", t).start())

    column = lax.broadcasted_iota(jnp.int32, (16, LANES), 1)
    half = LANES // 2
    total_log[me_t] = jnp.zeros(total_log.shape[1:], f32)
    for c in range(CHUNKS):
        stat_in[c, me_t] = stat[c, me_t]
        other_tensor(lambda t, c=c: send(
            stat.at[c, t], stat_in.at[c, t], rs_s.at[c, t], rs_r.at[c, t], "tensor", t).wait_recv())
        total = stat_in[c, 0]
        for t in range(1, nt):
            total = total + stat_in[c, t]
        norm = lax.rsqrt(total[per * 16:] / full_width + epsilon)
        summary = jnp.zeros((16, LANES), f32)
        all_logits = []
        for gl in range(per):
            g = c * per + gl
            logits = total[gl * 16:(gl + 1) * 16] * norm[gl:gl + 1]
            all_logits.append(logits)
            peak = jnp.max(logits, axis=1, keepdims=True)
            powers = jnp.exp(logits - peak)
            csum = jnp.sum(powers, axis=1, keepdims=True)
            wbuf[c, me_t, gl] = (powers * norm[gl:gl + 1]).astype(bf16)
            summary = jnp.where(column == g, peak, jnp.where(column == half + g, csum, summary))
        sbuf[c, me_t] = summary[:8] + pltpu.roll(summary[8:], LANES // 4, 1)
        other_tensor(lambda t, c=c: send(
            sbuf.at[c, me_t], sbuf.at[c, me_t], as_s.at[c, t], as_r.at[c, me_t], "tensor", t).start())
        other_tensor(lambda t, c=c: send(
            wbuf.at[c, me_t], wbuf.at[c, me_t], ag_s.at[c, t], ag_r.at[c, me_t], "tensor", t).start())
        for gl in range(per):
            g = c * per + gl
            logits = all_logits[gl]
            row_peak = jnp.max(logits, axis=0, keepdims=True)
            row_powers = jnp.exp(logits - row_peak)
            row_sum = jnp.sum(row_powers, axis=0, keepdims=True)
            combine[me_t, g] = (row_powers / row_sum).astype(bf16)
            total_log[me_t, g:g + 1, :] = row_peak + jnp.log(row_sum)

    fold = LANES // 4
    lane = lax.broadcasted_iota(jnp.int32, (8, LANES), 1)

    def slot_column(tile, g):
        low = jnp.sum(jnp.where(lane == g, tile, 0.0), axis=1, keepdims=True)
        high = jnp.sum(jnp.where(lane == fold + g, tile, 0.0), axis=1, keepdims=True)
        return jnp.concatenate([low, high], axis=0)

    for c in range(CHUNKS):
        other_tensor(lambda t, c=c: send(
            sbuf.at[c, t], sbuf.at[c, t], as_s.at[c, t], as_r.at[c, t], "tensor", t).wait_recv())
        peak = sbuf[c, 0]
        for q in range(1, nt):
            peak = jnp.maximum(peak, sbuf[c, q])
        factor = [jnp.exp(sbuf[c, q] - peak) for q in range(nt)]
        csum = factor[0] * pltpu.roll(sbuf[c, 0], half, 1)
        for q in range(1, nt):
            csum = csum + factor[q] * pltpu.roll(sbuf[c, q], half, 1)
        place = lane % fold
        mine = jnp.logical_and(lane < half, jnp.logical_and(place >= c * per, place < (c + 1) * per))
        stats[c, me_d] = jnp.where(mine, peak, 0.0) + pltpu.roll(jnp.where(mine, csum, 0.0), half, 1)
        other_owners(lambda j, c=c: send(
            stats.at[c, me_d], stats.at[c, me_d], st_s.at[c, j], st_r.at[c, me_d], "dp", j).start())
        other_tensor(lambda t, c=c: send(
            wbuf.at[c, t], wbuf.at[c, t], ag_s.at[c, t], ag_r.at[c, t], "tensor", t).wait_recv())

        def weigh(gl, carry, c=c, factor=factor):
            g = c * per + gl
            summed = jnp.zeros((16, width), f32)
            for q in range(nt):
                summed = summed + slot_column(factor[q], g) * lax.dot_general(
                    wbuf[c, q, gl], tok[g, q * quarter:(q + 1) * quarter, :], NN,
                    preferred_element_type=f32)
            for j in range(owners):
                pbuf[c, j, gl] = summed[:, j * LANES:(j + 1) * LANES].astype(bf16)
            return carry
        lax.fori_loop(0, per, weigh, 0)
        other_owners(lambda j, c=c: send(
            pbuf.at[c, j], rbuf.at[c, me_d], pr_s.at[c, j], pr_r.at[c, me_d], "dp", j).start())

    def spread_matrix(chunks, flip):
        shape = (nt * chunks * ROWS, chunks * per * 16)
        a = lax.broadcasted_iota(jnp.int32, shape[::-1] if flip else shape, 1 if flip else 0)
        b = lax.broadcasted_iota(jnp.int32, shape[::-1] if flip else shape, 0 if flip else 1)
        k, c, q = a // (chunks * ROWS), (a // ROWS) % chunks, a % ROWS
        source = (c * per + q // SLOTS) * 16 + k * SLOTS + q % SLOTS
        hit = jnp.logical_and(q < per * SLOTS, source == b)
        return jnp.where(hit, 1.0, 0.0).astype(bf16)

    spread = spread_matrix(1, False)
    gather = spread_matrix(CHUNKS, True)

    def reduce_slots():
        for c in range(CHUNKS):
            other_dp(lambda d, c=c: send(
                stats.at[c, d], stats.at[c, d], st_s.at[c, 0], st_r.at[c, d], "dp", d).wait_recv())
            peak = stats[c, 0]
            for i in range(1, nd):
                peak = jnp.maximum(peak, stats[c, i])
            factor = [jnp.exp(stats[c, i] - peak) for i in range(nd)]
            den = factor[0] * pltpu.roll(stats[c, 0], half, 1)
            for i in range(1, nd):
                den = den + factor[i] * pltpu.roll(stats[c, i], half, 1)
            scale = [f / den for f in factor]
            other_dp(lambda d, c=c: send(
                pbuf.at[c, 0], rbuf.at[c, d], pr_s.at[c, 0], pr_r.at[c, d], "dp", d).wait_recv())
            rbuf[c, me_d] = pbuf[c, me_d]
            rows = []
            for gl in range(per):
                g = c * per + gl
                acc = jnp.zeros((16, LANES), f32)
                for i in range(nd):
                    column_scale = jnp.concatenate(
                        [scale[i][:, g:g + 1], scale[i][:, fold + g:fold + g + 1]], axis=0)
                    acc = acc + column_scale * rbuf[c, i, gl].astype(f32)
                rows.append(acc.astype(bf16))
            slot_in = jnp.concatenate(rows, axis=0)
            moved = lax.dot_general(spread, slot_in, NN, preferred_element_type=f32).astype(bf16)
            for k in range(nt):
                abuf[c, k] = moved[k * ROWS:(k + 1) * ROWS]
            zin[c, me_t] = abuf[c, me_t]
            other_tensor(lambda t, c=c: send(
                abuf.at[c, t], zin.at[c, me_t], az_s.at[c, t], az_r.at[c, me_t], "tensor", t).start())
            other_tensor(lambda t, c=c: send(
                abuf.at[c, t], zin.at[c, t], az_s.at[c, t], az_r.at[c, t], "tensor", t).wait_recv())
            xin[me_d, c] = zin[c]
            other_dp(lambda d, c=c: send(
                zin.at[c], xin.at[me_d, c], ax_s.at[c, d], ax_r.at[c, me_d], "dp", d).start())
    if_owner(reduce_slots)

    other_tensor(lambda t: send(
        combine.at[me_t], combine.at[me_t], cb_s.at[t], cb_r.at[me_t], "tensor", t).start())
    other_tensor(lambda t: send(
        total_log.at[me_t], total_log.at[me_t], tb_s.at[t], tb_r.at[me_t], "tensor", t).start())

    for c in range(CHUNKS):
        other_tensor(lambda t, c=c: send(
            stat.at[c, t], stat_in.at[c, t], rs_s.at[c, t], rs_r.at[c, t], "tensor", t).wait_send())
        other_tensor(lambda t, c=c: send(
            wbuf.at[c, me_t], wbuf.at[c, me_t], ag_s.at[c, t], ag_r.at[c, t], "tensor", t).wait_send())
        other_tensor(lambda t, c=c: send(
            sbuf.at[c, me_t], sbuf.at[c, me_t], as_s.at[c, t], as_r.at[c, t], "tensor", t).wait_send())
        other_owners(lambda j, c=c: send(
            pbuf.at[c, j], rbuf.at[c, j], pr_s.at[c, j], pr_r.at[c, j], "dp", j).wait_send())
        other_owners(lambda j, c=c: send(
            stats.at[c, me_d], stats.at[c, me_d], st_s.at[c, j], st_r.at[c, j], "dp", j).wait_send())
    other_tensor(lambda t: send(
        combine.at[me_t], combine.at[t], cb_s.at[t], cb_r.at[t], "tensor", t).wait_send())
    other_tensor(lambda t: send(
        total_log.at[me_t], total_log.at[t], tb_s.at[t], tb_r.at[t], "tensor", t).wait_send())
    for m in (0, 1):
        for p in range(WPARTS):
            weight_copy(m, p).wait()
    pairs = owners // 2
    fc = 256 if hidden_here % 256 == 0 else hidden_here
    gate_acc[...] = jnp.zeros(gate_acc.shape, f32)
    up_acc[...] = jnp.zeros(up_acc.shape, f32)

    def feature_part(k, carry):
        p = lax.rem(k + me_d // 2, pairs)
        for h in range(2):
            j = 2 * p + h

            @pl.when(j != me_d)
            def _():
                for c in range(CHUNKS):
                    send(zin.at[c], xin.at[j, c], ax_s.at[c, 0], ax_r.at[c, j], "dp", j).wait_recv()
        xs = []
        for t in range(nt):
            xs.append(jnp.concatenate([
                jnp.concatenate([xin[2 * p + h, c, t] for c in range(CHUNKS)], axis=0)
                for h in range(2)], axis=1))
        for f in range(hidden_here // fc):
            rows = slice(f * fc, (f + 1) * fc)
            for w, acc in ((wg, gate_acc), (wu, up_acc)):
                part = acc[:, rows]
                for t in range(nt):
                    cols = pl.ds(pl.multiple_of(t * width + p * 2 * LANES, 2 * LANES), 2 * LANES)
                    part = part + lax.dot_general(xs[t], w[rows, cols], NT, preferred_element_type=f32)
                acc[:, rows] = part
        return carry
    lax.fori_loop(0, pairs, feature_part, 0)
    gate = gate_acc[...]
    hidden[...] = (gate / (1.0 + jnp.exp(-gate)) * up_acc[...]).astype(bf16)

    for p in range(WPARTS):
        weight_copy(2, p).wait()

    def down_part(k, carry):
        p = lax.rem(k + me_d // 2 + 1, pairs)
        for t in range(nt):
            cols = pl.ds(pl.multiple_of(t * width + p * 2 * LANES, 2 * LANES), 2 * LANES)
            out = lax.dot_general(hidden[...], wd[:, cols], NN, preferred_element_type=f32)
            obuf[2 * p, t] = out[:, :LANES].astype(bf16)
            obuf[2 * p + 1, t] = out[:, LANES:].astype(bf16)
        for h in range(2):
            j = 2 * p + h

            @pl.when(j != me_d)
            def _():
                send(obuf.at[j], oin.at[me_d], or_s.at[j], or_r.at[me_d], "dp", j).start()
        return carry
    lax.fori_loop(0, pairs, down_part, 0)

    def drain_inputs():
        for c in range(CHUNKS):
            other_tensor(lambda t, c=c: send(
                abuf.at[c, t], zin.at[c, t], az_s.at[c, t], az_r.at[c, t], "tensor", t).wait_send())
            other_dp(lambda d, c=c: send(
                zin.at[c], xin.at[0, c], ax_s.at[c, d], ax_r.at[c, d], "dp", d).wait_send())
    if_owner(drain_inputs)
    other_tensor(lambda t: send(
        combine.at[t], combine.at[t], cb_s.at[t], cb_r.at[t], "tensor", t).wait_recv())
    other_tensor(lambda t: send(
        total_log.at[t], total_log.at[t], tb_s.at[t], tb_r.at[t], "tensor", t).wait_recv())
    combine_write = pltpu.make_async_copy(combine, combine_out, out_sem.at[0])
    total_write = pltpu.make_async_copy(total_log, total_out, out_sem.at[1])
    combine_write.start()
    total_write.start()

    def reduce_outputs():
        oin[me_d] = obuf[me_d]
        other_dp(lambda d: send(
            obuf.at[0], oin.at[d], or_s.at[0], or_r.at[d], "dp", d).wait_recv())
        for t in range(nt):
            acc = oin[0, t].astype(f32)
            for i in range(1, nd):
                acc = acc + oin[i, t].astype(f32)
            bbuf[t] = acc.astype(bf16)
        zout[me_t] = bbuf[me_t]
        other_tensor(lambda t: send(
            bbuf.at[t], zout.at[me_t], bz_s.at[t], bz_r.at[me_t], "tensor", t).start())
        other_tensor(lambda t: send(
            bbuf.at[t], zout.at[t], bz_s.at[t], bz_r.at[t], "tensor", t).wait_recv())
        rows = jnp.concatenate([zout[k] for k in range(nt)], axis=0)
        mine_out[...] = lax.dot_general(
            gather, rows, NN, preferred_element_type=f32).astype(bf16)
        other_dp(lambda d: send(
            mine_out, window_out.at[me_d], bx_s.at[d], bx_r.at[me_d], "dp", d).start())
        pltpu.make_async_copy(mine_out, window_out.at[me_d], out_sem.at[2]).start()
    if_owner(reduce_outputs)
    other_owners(lambda j: send(
        mine_out, window_out.at[j], bx_s.at[0], bx_r.at[j], "dp", j).wait_recv())

    other_owners(lambda j: send(
        obuf.at[j], oin.at[j], or_s.at[j], or_r.at[j], "dp", j).wait_send())

    def drain():
        other_tensor(lambda t: send(
            bbuf.at[t], zout.at[t], bz_s.at[t], bz_r.at[t], "tensor", t).wait_send())
        other_dp(lambda d: send(
            mine_out, window_out.at[me_d], bx_s.at[d], bx_r.at[d], "dp", d).wait_send())
        pltpu.make_async_copy(mine_out, window_out.at[me_d], out_sem.at[2]).wait()
    if_owner(drain)
    combine_write.wait()
    total_write.wait()


def mix_kernel(combine_in, window_in, total_in, mixed, total_out, combine, window, total, held, in_sem, sem):
    loads = [
        pltpu.make_async_copy(combine_in, combine, in_sem.at[0]),
        pltpu.make_async_copy(window_in, window, in_sem.at[1]),
        pltpu.make_async_copy(total_in, total, in_sem.at[2]),
    ]
    for load in loads:
        load.start()
    nt, groups = combine.shape[:2]
    owners, quarter = window.shape[0], combine.shape[3]

    def copy(g):
        return pltpu.make_async_copy(held.at[g], mixed.at[g], sem.at[g])

    for load in loads:
        load.wait()

    def mix_group(g, carry):
        slots = jnp.concatenate([window[j, g] for j in range(owners)], axis=1)
        rows = jnp.concatenate([combine[q, g] for q in range(nt)], axis=1)
        held[g] = lax.dot_general(
            rows, slots, (((0,), (0,)), ((), ())), preferred_element_type=f32).astype(bf16)
        copy(g).start()
        return carry
    lax.fori_loop(0, groups, mix_group, 0)
    for q in range(nt):
        total_out[:, q * quarter:(q + 1) * quarter] = total[q, :groups, :]
    for g in range(groups):
        copy(g).wait()


def per_device(tokens, router, w_gate, w_up, w_down):
    nd, nt = lax.axis_size("dp"), lax.axis_size("tensor")
    groups, count, width = tokens.shape
    hidden_here, full = w_gate.shape[1:]
    slots = router.shape[0]
    owners = width // LANES
    quarter = count // nt
    per = groups // CHUNKS
    srows = per * 16 + 8
    VM, DMA = pltpu.VMEM, pltpu.SemaphoreType.DMA
    any_spec = pl.BlockSpec(memory_space=pl.ANY)
    vmem_spec = pl.BlockSpec(memory_space=pltpu.VMEM)
    hbm_spec = pl.BlockSpec(memory_space=pltpu.HBM)
    window, combine, total = pl.pallas_call(
        functools.partial(dispatch_kernel, nd, nt),
        out_shape=(
            jax.ShapeDtypeStruct((owners, groups * slots, LANES), bf16),
            jax.ShapeDtypeStruct((nt, groups, slots, quarter), bf16),
            jax.ShapeDtypeStruct((nt, 8, quarter), f32),
        ),
        in_specs=[any_spec, vmem_spec, any_spec, any_spec, any_spec],
        out_specs=(hbm_spec, hbm_spec, hbm_spec),
        scratch_shapes=[
            VM((groups, count, width), bf16),
            VM((hidden_here, full), bf16),
            VM((hidden_here, full), bf16),
            VM((hidden_here, full), bf16),
            VM((CHUNKS, nt, srows, quarter), f32),
            VM((CHUNKS, nt, srows, quarter), f32),
            VM((CHUNKS, nt, per, slots, quarter), bf16),
            VM((CHUNKS, nt, 8, LANES), f32),
            VM((CHUNKS, nd, 8, LANES), f32),
            VM((CHUNKS, owners, per, slots, LANES), bf16),
            VM((CHUNKS, nd, per, slots, LANES), bf16),
            VM((CHUNKS, nt, ROWS, LANES), bf16),
            VM((CHUNKS, nt, ROWS, LANES), bf16),
            VM((owners, CHUNKS, nt, ROWS, LANES), bf16),
            VM((PAD, hidden_here), f32),
            VM((PAD, hidden_here), f32),
            VM((PAD, hidden_here), bf16),
            VM((owners, nt, PAD, LANES), bf16),
            VM((nd, nt, PAD, LANES), bf16),
            VM((nt, PAD, LANES), bf16),
            VM((nt, PAD, LANES), bf16),
            VM((nt, groups, slots, quarter), bf16),
            VM((nt, 8, quarter), f32),
            VM((groups * slots, LANES), bf16),
            DMA((groups,)), DMA((3, WPARTS)), DMA((3,)),
            DMA((CHUNKS, nt)), DMA((CHUNKS, nt)), DMA((CHUNKS, nt)), DMA((CHUNKS, nt)),
            DMA((CHUNKS, nt)), DMA((CHUNKS, nt)), DMA((nt,)), DMA((nt,)), DMA((nt,)), DMA((nt,)),
            DMA((CHUNKS, owners)), DMA((CHUNKS, nd)), DMA((CHUNKS, owners)), DMA((CHUNKS, nd)),
            DMA((CHUNKS, nt)), DMA((CHUNKS, nt)), DMA((CHUNKS, nd)), DMA((CHUNKS, owners)),
            DMA((owners,)), DMA((nd,)), DMA((nt,)), DMA((nt,)), DMA((nd,)), DMA((owners,)),
        ],
        compiler_params=pltpu.CompilerParams(
            collective_id=0, has_side_effects=True, vmem_limit_bytes=58 * 1024 * 1024),
        name="dispatch",
    )(tokens, router, w_gate[0], w_up[0], w_down[0])
    window = window.reshape(owners, groups, slots, LANES)
    mixed, log_total = pl.pallas_call(
        mix_kernel,
        out_shape=(
            jax.ShapeDtypeStruct((groups, count, width), bf16),
            jax.ShapeDtypeStruct((groups, count), f32),
        ),
        in_specs=[hbm_spec, hbm_spec, hbm_spec],
        out_specs=(any_spec, vmem_spec),
        scratch_shapes=[
            VM(combine.shape, bf16), VM(window.shape, bf16), VM(total.shape, f32),
            VM((groups, count, width), bf16), DMA((3,)), DMA((groups,)),
        ],
        compiler_params=pltpu.CompilerParams(vmem_limit_bytes=60 * 1024 * 1024),
        name="mix",
    )(combine, window, total)
    return (mixed, log_total)


def solution(mesh):
    in_specs = (
        P(None, "dp", "tensor"),
        P(None, "tensor"),
        P("tensor", "dp", None),
        P("tensor", "dp", None),
        P("tensor", "dp", None),
    )
    out_specs = (P(None, "dp", "tensor"), P(None, "dp"))
    return jax.shard_map(
        per_device, mesh=mesh, in_specs=in_specs, out_specs=out_specs, check_vma=False
    )
```

```python
import functools

import jax
import jax.numpy as jnp
from jax import lax
from jax.experimental import pallas as pl
from jax.experimental.pallas import tpu as pltpu
from jax.sharding import PartitionSpec as P

SLOTS = 4
ROWS = 16
LANES = 128
CHUNKS = 2
PAD = ROWS * CHUNKS
WPARTS = 7
epsilon = 1e-05
f32 = jnp.float32
bf16 = jnp.bfloat16
MESH = pl.DeviceIdType.MESH
NT = (((1,), (1,)), ((), ()))
NN = (((1,), (0,)), ((), ()))


def dispatch_kernel(
    nd, nt, tokens, router, w_gate, w_up, w_down,
    window_out, combine_out, total_out,
    tok, wg, wu, wd, stat, stat_in, wbuf, sbuf, stats, pbuf, rbuf, abuf, zin, xin, gate_acc, up_acc, hidden,
    obuf, oin, bbuf, zout, combine, total_log, mine_out,
    tok_sem, w_sem, out_sem,
    rs_s, rs_r, ag_s, ag_r, as_s, as_r, cb_s, cb_r, tb_s, tb_r, st_s, st_r, pr_s, pr_r, az_s, az_r, ax_s, ax_r,
    or_s, or_r, bz_s, bz_r, bx_s, bx_r,
):
    me_d, me_t = lax.axis_index("dp"), lax.axis_index("tensor")
    groups, count, width = tok.shape
    owners = width // LANES
    quarter = count // nt
    per = groups // CHUNKS
    full_width = width * nt
    hidden_here = wg.shape[0]
    wrows = hidden_here // WPARTS
    is_owner_all = nd == owners

    def token_copy(g):
        return pltpu.make_async_copy(tokens.at[g], tok.at[g], tok_sem.at[g])

    def weight_copy(m, p):
        src, dst = ((w_gate, wg), (w_up, wu), (w_down, wd))[m]
        rows = pl.ds(p * wrows, wrows)
        return pltpu.make_async_copy(src.at[rows, :], dst.at[rows, :], w_sem.at[m, p])

    def ring(me, n, fn):
        def step(k, c):
            fn(lax.rem(me + k, n))
            return c
        lax.fori_loop(1, n, step, 0)

    def other_tensor(fn):
        ring(me_t, nt, fn)

    def other_dp(fn):
        ring(me_d, nd, fn)

    def other_owners(fn):
        if is_owner_all:
            ring(me_d, nd, fn)
        else:
            def step(j, c):
                pl.when(j != me_d)(functools.partial(fn, j))
                return c
            lax.fori_loop(0, owners, step, 0)

    def if_owner(fn):
        if is_owner_all:
            fn()
        else:
            pl.when(me_d < owners)(fn)

    def send(src, dst, s, r, axis, to):
        return pltpu.make_async_remote_copy(
            src_ref=src, dst_ref=dst, send_sem=s, recv_sem=r,
            device_id={axis: to}, device_id_type=MESH)

    for g in range(groups):
        token_copy(g).start()
    pieces = [(m, p) for m in range(3) for p in range(WPARTS)]

    def start_weights(n):
        for m, p in pieces[:n]:
            weight_copy(m, p).start(priority=1)
        del pieces[:n]

    barrier = pltpu.get_barrier_semaphore()
    other_tensor(lambda t: pl.semaphore_signal(
        barrier, inc=1, device_id={"tensor": t}, device_id_type=MESH))
    other_dp(lambda d: pl.semaphore_signal(
        barrier, inc=1, device_id={"dp": d}, device_id_type=MESH))

    router_rows = router[...]

    for c in range(CHUNKS):
        def partial_logits(gl, carry, c=c):
            g = c * per + gl
            token_copy(g).wait()
            raw = lax.dot_general(router_rows, tok[g], NT, preferred_element_type=f32)
            rows = pl.ds(pl.multiple_of(gl * 16, 16), 16)
            for q in range(nt):
                stat[c, q, rows, :] = raw[:, q * quarter:(q + 1) * quarter]
                acc = jnp.zeros((quarter, LANES), f32)
                for b in range(owners):
                    part = tok[g, q * quarter:(q + 1) * quarter, b * LANES:(b + 1) * LANES].astype(f32)
                    acc = acc + part * part
                stat[c, q, pl.ds(per * 16 + gl, 1), :] = jnp.sum(acc.T, axis=0, keepdims=True)
            return carry
        stat[c, :, per * 16:, :] = jnp.zeros((nt, 8, LANES), f32)
        lax.fori_loop(0, per, partial_logits, 0)
        if c == 0:
            pl.semaphore_wait(barrier, nt - 1 + nd - 1)
        other_tensor(lambda t, c=c: send(
            stat.at[c, t], stat_in.at[c, me_t], rs_s.at[c, t], rs_r.at[c, me_t], "tensor", t).start())
        start_weights(3)

    column = lax.broadcasted_iota(jnp.int32, (16, LANES), 1)
    half = LANES // 2
    total_log[me_t] = jnp.zeros(total_log.shape[1:], f32)
    for c in range(CHUNKS):
        stat_in[c, me_t] = stat[c, me_t]
        other_tensor(lambda t, c=c: send(
            stat.at[c, t], stat_in.at[c, t], rs_s.at[c, t], rs_r.at[c, t], "tensor", t).wait_recv())
        total = stat_in[c, 0]
        for t in range(1, nt):
            total = total + stat_in[c, t]
        norm = lax.rsqrt(total[per * 16:] / full_width + epsilon)
        summary = jnp.zeros((16, LANES), f32)
        all_logits = []
        for gl in range(per):
            g = c * per + gl
            logits = total[gl * 16:(gl + 1) * 16] * norm[gl:gl + 1]
            all_logits.append(logits)
            peak = jnp.max(logits, axis=1, keepdims=True)
            powers = jnp.exp(logits - peak)
            csum = jnp.sum(powers, axis=1, keepdims=True)
            wbuf[c, me_t, gl] = (powers * norm[gl:gl + 1]).astype(bf16)
            summary = jnp.where(column == g, peak, jnp.where(column == half + g, csum, summary))
        sbuf[c, me_t] = summary[:8] + pltpu.roll(summary[8:], LANES // 4, 1)
        other_tensor(lambda t, c=c: send(
            sbuf.at[c, me_t], sbuf.at[c, me_t], as_s.at[c, t], as_r.at[c, me_t], "tensor", t).start())
        other_tensor(lambda t, c=c: send(
            wbuf.at[c, me_t], wbuf.at[c, me_t], ag_s.at[c, t], ag_r.at[c, me_t], "tensor", t).start())
        start_weights(3 if c == 0 else 4)
        for gl in range(per):
            g = c * per + gl
            logits = all_logits[gl]
            row_peak = jnp.max(logits, axis=0, keepdims=True)
            row_powers = jnp.exp(logits - row_peak)
            row_sum = jnp.sum(row_powers, axis=0, keepdims=True)
            combine[me_t, g] = (row_powers / row_sum).astype(bf16)
            total_log[me_t, g:g + 1, :] = row_peak + jnp.log(row_sum)

    fold = LANES // 4
    lane = lax.broadcasted_iota(jnp.int32, (8, LANES), 1)

    def slot_column(tile, g):
        low = jnp.sum(jnp.where(lane == g, tile, 0.0), axis=1, keepdims=True)
        high = jnp.sum(jnp.where(lane == fold + g, tile, 0.0), axis=1, keepdims=True)
        return jnp.concatenate([low, high], axis=0)

    for c in range(CHUNKS):
        other_tensor(lambda t, c=c: send(
            sbuf.at[c, t], sbuf.at[c, t], as_s.at[c, t], as_r.at[c, t], "tensor", t).wait_recv())
        peak = sbuf[c, 0]
        for q in range(1, nt):
            peak = jnp.maximum(peak, sbuf[c, q])
        factor = [jnp.exp(sbuf[c, q] - peak) for q in range(nt)]
        csum = factor[0] * pltpu.roll(sbuf[c, 0], half, 1)
        for q in range(1, nt):
            csum = csum + factor[q] * pltpu.roll(sbuf[c, q], half, 1)
        place = lane % fold
        mine = jnp.logical_and(lane < half, jnp.logical_and(place >= c * per, place < (c + 1) * per))
        stats[c, me_d] = jnp.where(mine, peak, 0.0) + pltpu.roll(jnp.where(mine, csum, 0.0), half, 1)
        other_owners(lambda j, c=c: send(
            stats.at[c, me_d], stats.at[c, me_d], st_s.at[c, j], st_r.at[c, me_d], "dp", j).start())
        other_tensor(lambda t, c=c: send(
            wbuf.at[c, t], wbuf.at[c, t], ag_s.at[c, t], ag_r.at[c, t], "tensor", t).wait_recv())

        def weigh(gl, carry, c=c, factor=factor):
            g = c * per + gl
            summed = jnp.zeros((16, width), f32)
            for q in range(nt):
                summed = summed + slot_column(factor[q], g) * lax.dot_general(
                    wbuf[c, q, gl], tok[g, q * quarter:(q + 1) * quarter, :], NN,
                    preferred_element_type=f32)
            for j in range(owners):
                pbuf[c, j, gl] = summed[:, j * LANES:(j + 1) * LANES].astype(bf16)
            return carry
        lax.fori_loop(0, per, weigh, 0)
        other_owners(lambda j, c=c: send(
            pbuf.at[c, j], rbuf.at[c, me_d], pr_s.at[c, j], pr_r.at[c, me_d], "dp", j).start())
        start_weights(2 if c == 0 else 3)

    def spread_matrix(chunks, flip):
        shape = (nt * chunks * ROWS, chunks * per * 16)
        a = lax.broadcasted_iota(jnp.int32, shape[::-1] if flip else shape, 1 if flip else 0)
        b = lax.broadcasted_iota(jnp.int32, shape[::-1] if flip else shape, 0 if flip else 1)
        k, c, q = a // (chunks * ROWS), (a // ROWS) % chunks, a % ROWS
        source = (c * per + q // SLOTS) * 16 + k * SLOTS + q % SLOTS
        hit = jnp.logical_and(q < per * SLOTS, source == b)
        return jnp.where(hit, 1.0, 0.0).astype(bf16)

    spread = spread_matrix(1, False)
    gather = spread_matrix(CHUNKS, True)

    def reduce_slots():
        for c in range(CHUNKS):
            other_dp(lambda d, c=c: send(
                stats.at[c, d], stats.at[c, d], st_s.at[c, 0], st_r.at[c, d], "dp", d).wait_recv())
            peak = stats[c, 0]
            for i in range(1, nd):
                peak = jnp.maximum(peak, stats[c, i])
            factor = [jnp.exp(stats[c, i] - peak) for i in range(nd)]
            den = factor[0] * pltpu.roll(stats[c, 0], half, 1)
            for i in range(1, nd):
                den = den + factor[i] * pltpu.roll(stats[c, i], half, 1)
            scale = [f / den for f in factor]
            other_dp(lambda d, c=c: send(
                pbuf.at[c, 0], rbuf.at[c, d], pr_s.at[c, 0], pr_r.at[c, d], "dp", d).wait_recv())
            rbuf[c, me_d] = pbuf[c, me_d]
            rows = []
            for gl in range(per):
                g = c * per + gl
                acc = jnp.zeros((16, LANES), f32)
                for i in range(nd):
                    column_scale = jnp.concatenate(
                        [scale[i][:, g:g + 1], scale[i][:, fold + g:fold + g + 1]], axis=0)
                    acc = acc + column_scale * rbuf[c, i, gl].astype(f32)
                rows.append(acc.astype(bf16))
            slot_in = jnp.concatenate(rows, axis=0)
            moved = lax.dot_general(spread, slot_in, NN, preferred_element_type=f32).astype(bf16)
            for k in range(nt):
                abuf[c, k] = moved[k * ROWS:(k + 1) * ROWS]
            zin[c, me_t] = abuf[c, me_t]
            other_tensor(lambda t, c=c: send(
                abuf.at[c, t], zin.at[c, me_t], az_s.at[c, t], az_r.at[c, me_t], "tensor", t).start())
            other_tensor(lambda t, c=c: send(
                abuf.at[c, t], zin.at[c, t], az_s.at[c, t], az_r.at[c, t], "tensor", t).wait_recv())
            xin[me_d, c] = zin[c]
            other_dp(lambda d, c=c: send(
                zin.at[c], xin.at[me_d, c], ax_s.at[c, d], ax_r.at[c, me_d], "dp", d).start())
    if_owner(reduce_slots)
    start_weights(len(pieces))

    other_tensor(lambda t: send(
        combine.at[me_t], combine.at[me_t], cb_s.at[t], cb_r.at[me_t], "tensor", t).start())
    other_tensor(lambda t: send(
        total_log.at[me_t], total_log.at[me_t], tb_s.at[t], tb_r.at[me_t], "tensor", t).start())

    for c in range(CHUNKS):
        other_tensor(lambda t, c=c: send(
            stat.at[c, t], stat_in.at[c, t], rs_s.at[c, t], rs_r.at[c, t], "tensor", t).wait_send())
        other_tensor(lambda t, c=c: send(
            wbuf.at[c, me_t], wbuf.at[c, me_t], ag_s.at[c, t], ag_r.at[c, t], "tensor", t).wait_send())
        other_tensor(lambda t, c=c: send(
            sbuf.at[c, me_t], sbuf.at[c, me_t], as_s.at[c, t], as_r.at[c, t], "tensor", t).wait_send())
        other_owners(lambda j, c=c: send(
            pbuf.at[c, j], rbuf.at[c, j], pr_s.at[c, j], pr_r.at[c, j], "dp", j).wait_send())
        other_owners(lambda j, c=c: send(
            stats.at[c, me_d], stats.at[c, me_d], st_s.at[c, j], st_r.at[c, j], "dp", j).wait_send())
    other_tensor(lambda t: send(
        combine.at[me_t], combine.at[t], cb_s.at[t], cb_r.at[t], "tensor", t).wait_send())
    other_tensor(lambda t: send(
        total_log.at[me_t], total_log.at[t], tb_s.at[t], tb_r.at[t], "tensor", t).wait_send())
    for m in (0, 1):
        for p in range(WPARTS):
            weight_copy(m, p).wait()
    pairs = owners // 2
    fc = 256 if hidden_here % 256 == 0 else hidden_here
    gate_acc[...] = jnp.zeros(gate_acc.shape, f32)
    up_acc[...] = jnp.zeros(up_acc.shape, f32)

    def feature_part(k, carry):
        p = lax.rem(k + me_d // 2, pairs)
        for h in range(2):
            j = 2 * p + h

            @pl.when(j != me_d)
            def _():
                for c in range(CHUNKS):
                    send(zin.at[c], xin.at[j, c], ax_s.at[c, 0], ax_r.at[c, j], "dp", j).wait_recv()
        xs = []
        for t in range(nt):
            xs.append(jnp.concatenate([
                jnp.concatenate([xin[2 * p + h, c, t] for c in range(CHUNKS)], axis=0)
                for h in range(2)], axis=1))
        for f in range(hidden_here // fc):
            rows = slice(f * fc, (f + 1) * fc)
            for w, acc in ((wg, gate_acc), (wu, up_acc)):
                part = acc[:, rows]
                for t in range(nt):
                    cols = pl.ds(pl.multiple_of(t * width + p * 2 * LANES, 2 * LANES), 2 * LANES)
                    part = part + lax.dot_general(xs[t], w[rows, cols], NT, preferred_element_type=f32)
                acc[:, rows] = part
        return carry
    lax.fori_loop(0, pairs, feature_part, 0)
    gate = gate_acc[...]
    hidden[...] = (gate / (1.0 + jnp.exp(-gate)) * up_acc[...]).astype(bf16)

    for p in range(WPARTS):
        weight_copy(2, p).wait()

    def down_part(k, carry):
        p = lax.rem(k + me_d // 2 + 1, pairs)
        for t in range(nt):
            cols = pl.ds(pl.multiple_of(t * width + p * 2 * LANES, 2 * LANES), 2 * LANES)
            out = lax.dot_general(hidden[...], wd[:, cols], NN, preferred_element_type=f32)
            obuf[2 * p, t] = out[:, :LANES].astype(bf16)
            obuf[2 * p + 1, t] = out[:, LANES:].astype(bf16)
        for h in range(2):
            j = 2 * p + h

            @pl.when(j != me_d)
            def _():
                send(obuf.at[j], oin.at[me_d], or_s.at[j], or_r.at[me_d], "dp", j).start()
        return carry
    lax.fori_loop(0, pairs, down_part, 0)

    def drain_inputs():
        for c in range(CHUNKS):
            other_tensor(lambda t, c=c: send(
                abuf.at[c, t], zin.at[c, t], az_s.at[c, t], az_r.at[c, t], "tensor", t).wait_send())
            other_dp(lambda d, c=c: send(
                zin.at[c], xin.at[0, c], ax_s.at[c, d], ax_r.at[c, d], "dp", d).wait_send())
    if_owner(drain_inputs)
    other_tensor(lambda t: send(
        combine.at[t], combine.at[t], cb_s.at[t], cb_r.at[t], "tensor", t).wait_recv())
    other_tensor(lambda t: send(
        total_log.at[t], total_log.at[t], tb_s.at[t], tb_r.at[t], "tensor", t).wait_recv())
    combine_write = pltpu.make_async_copy(combine, combine_out, out_sem.at[0])
    total_write = pltpu.make_async_copy(total_log, total_out, out_sem.at[1])
    combine_write.start()
    total_write.start()

    def reduce_outputs():
        oin[me_d] = obuf[me_d]
        other_dp(lambda d: send(
            obuf.at[0], oin.at[d], or_s.at[0], or_r.at[d], "dp", d).wait_recv())
        for t in range(nt):
            acc = oin[0, t].astype(f32)
            for i in range(1, nd):
                acc = acc + oin[i, t].astype(f32)
            bbuf[t] = acc.astype(bf16)
        zout[me_t] = bbuf[me_t]
        other_tensor(lambda t: send(
            bbuf.at[t], zout.at[me_t], bz_s.at[t], bz_r.at[me_t], "tensor", t).start())
        other_tensor(lambda t: send(
            bbuf.at[t], zout.at[t], bz_s.at[t], bz_r.at[t], "tensor", t).wait_recv())
        rows = jnp.concatenate([zout[k] for k in range(nt)], axis=0)
        mine_out[...] = lax.dot_general(
            gather, rows, NN, preferred_element_type=f32).astype(bf16)
        other_dp(lambda d: send(
            mine_out, window_out.at[me_d], bx_s.at[d], bx_r.at[me_d], "dp", d).start())
        pltpu.make_async_copy(mine_out, window_out.at[me_d], out_sem.at[2]).start()
    if_owner(reduce_outputs)
    other_owners(lambda j: send(
        mine_out, window_out.at[j], bx_s.at[0], bx_r.at[j], "dp", j).wait_recv())

    other_owners(lambda j: send(
        obuf.at[j], oin.at[j], or_s.at[j], or_r.at[j], "dp", j).wait_send())

    def drain():
        other_tensor(lambda t: send(
            bbuf.at[t], zout.at[t], bz_s.at[t], bz_r.at[t], "tensor", t).wait_send())
        other_dp(lambda d: send(
            mine_out, window_out.at[me_d], bx_s.at[d], bx_r.at[d], "dp", d).wait_send())
        pltpu.make_async_copy(mine_out, window_out.at[me_d], out_sem.at[2]).wait()
    if_owner(drain)
    combine_write.wait()
    total_write.wait()


def mix_kernel(combine_in, window_in, total_in, mixed, total_out, combine, window, total, held, in_sem, sem):
    loads = [
        pltpu.make_async_copy(combine_in, combine, in_sem.at[0]),
        pltpu.make_async_copy(window_in, window, in_sem.at[1]),
        pltpu.make_async_copy(total_in, total, in_sem.at[2]),
    ]
    for load in loads:
        load.start()
    nt, groups = combine.shape[:2]
    owners, quarter = window.shape[0], combine.shape[3]

    def copy(g):
        return pltpu.make_async_copy(held.at[g], mixed.at[g], sem.at[g])

    for load in loads:
        load.wait()

    def mix_group(g, carry):
        slots = jnp.concatenate([window[j, g] for j in range(owners)], axis=1)
        rows = jnp.concatenate([combine[q, g] for q in range(nt)], axis=1)
        held[g] = lax.dot_general(
            rows, slots, (((0,), (0,)), ((), ())), preferred_element_type=f32).astype(bf16)
        copy(g).start()
        return carry
    lax.fori_loop(0, groups, mix_group, 0)
    for q in range(nt):
        total_out[:, q * quarter:(q + 1) * quarter] = total[q, :groups, :]
    for g in range(groups):
        copy(g).wait()


def per_device(tokens, router, w_gate, w_up, w_down):
    nd, nt = lax.axis_size("dp"), lax.axis_size("tensor")
    groups, count, width = tokens.shape
    hidden_here, full = w_gate.shape[1:]
    slots = router.shape[0]
    owners = width // LANES
    quarter = count // nt
    per = groups // CHUNKS
    srows = per * 16 + 8
    VM, DMA = pltpu.VMEM, pltpu.SemaphoreType.DMA
    any_spec = pl.BlockSpec(memory_space=pl.ANY)
    vmem_spec = pl.BlockSpec(memory_space=pltpu.VMEM)
    hbm_spec = pl.BlockSpec(memory_space=pltpu.HBM)
    window, combine, total = pl.pallas_call(
        functools.partial(dispatch_kernel, nd, nt),
        out_shape=(
            jax.ShapeDtypeStruct((owners, groups * slots, LANES), bf16),
            jax.ShapeDtypeStruct((nt, groups, slots, quarter), bf16),
            jax.ShapeDtypeStruct((nt, 8, quarter), f32),
        ),
        in_specs=[any_spec, vmem_spec, any_spec, any_spec, any_spec],
        out_specs=(hbm_spec, hbm_spec, hbm_spec),
        scratch_shapes=[
            VM((groups, count, width), bf16),
            VM((hidden_here, full), bf16),
            VM((hidden_here, full), bf16),
            VM((hidden_here, full), bf16),
            VM((CHUNKS, nt, srows, quarter), f32),
            VM((CHUNKS, nt, srows, quarter), f32),
            VM((CHUNKS, nt, per, slots, quarter), bf16),
            VM((CHUNKS, nt, 8, LANES), f32),
            VM((CHUNKS, nd, 8, LANES), f32),
            VM((CHUNKS, owners, per, slots, LANES), bf16),
            VM((CHUNKS, nd, per, slots, LANES), bf16),
            VM((CHUNKS, nt, ROWS, LANES), bf16),
            VM((CHUNKS, nt, ROWS, LANES), bf16),
            VM((owners, CHUNKS, nt, ROWS, LANES), bf16),
            VM((PAD, hidden_here), f32),
            VM((PAD, hidden_here), f32),
            VM((PAD, hidden_here), bf16),
            VM((owners, nt, PAD, LANES), bf16),
            VM((nd, nt, PAD, LANES), bf16),
            VM((nt, PAD, LANES), bf16),
            VM((nt, PAD, LANES), bf16),
            VM((nt, groups, slots, quarter), bf16),
            VM((nt, 8, quarter), f32),
            VM((groups * slots, LANES), bf16),
            DMA((groups,)), DMA((3, WPARTS)), DMA((3,)),
            DMA((CHUNKS, nt)), DMA((CHUNKS, nt)), DMA((CHUNKS, nt)), DMA((CHUNKS, nt)),
            DMA((CHUNKS, nt)), DMA((CHUNKS, nt)), DMA((nt,)), DMA((nt,)), DMA((nt,)), DMA((nt,)),
            DMA((CHUNKS, owners)), DMA((CHUNKS, nd)), DMA((CHUNKS, owners)), DMA((CHUNKS, nd)),
            DMA((CHUNKS, nt)), DMA((CHUNKS, nt)), DMA((CHUNKS, nd)), DMA((CHUNKS, owners)),
            DMA((owners,)), DMA((nd,)), DMA((nt,)), DMA((nt,)), DMA((nd,)), DMA((owners,)),
        ],
        compiler_params=pltpu.CompilerParams(
            collective_id=0, has_side_effects=True, vmem_limit_bytes=58 * 1024 * 1024),
        name="dispatch",
    )(tokens, router, w_gate[0], w_up[0], w_down[0])
    window = window.reshape(owners, groups, slots, LANES)
    mixed, log_total = pl.pallas_call(
        mix_kernel,
        out_shape=(
            jax.ShapeDtypeStruct((groups, count, width), bf16),
            jax.ShapeDtypeStruct((groups, count), f32),
        ),
        in_specs=[hbm_spec, hbm_spec, hbm_spec],
        out_specs=(any_spec, vmem_spec),
        scratch_shapes=[
            VM(combine.shape, bf16), VM(window.shape, bf16), VM(total.shape, f32),
            VM((groups, count, width), bf16), DMA((3,)), DMA((groups,)),
        ],
        compiler_params=pltpu.CompilerParams(vmem_limit_bytes=60 * 1024 * 1024),
        name="mix",
    )(combine, window, total)
    return (mixed, log_total)


def solution(mesh):
    in_specs = (
        P(None, "dp", "tensor"),
        P(None, "tensor"),
        P("tensor", "dp", None),
        P("tensor", "dp", None),
        P("tensor", "dp", None),
    )
    out_specs = (P(None, "dp", "tensor"), P(None, "dp"))
    return jax.shard_map(
        per_device, mesh=mesh, in_specs=in_specs, out_specs=out_specs, check_vma=False
    )
```
